32 devices in a mesh: groups: 2 (over x), dp: 2 (over core), mp: 8 (over z, y).
Axes of the slice: x: 2, y: 2, z: 4, core: 2. Of those that a mesh axis runs over, the one named last changes fastest.
Arguments:
- tokens: bfloat16 [16384, 8192], P(('groups', 'dp'), 'mp'), parts along dimension 0, may hold values from -6 to 6
- frozen_weight: bfloat16 [8192, 1024], P('mp'), may hold values from -0.09375 to 0.09375
- cotangent: bfloat16 [16384, 1024], P(('groups', 'dp'), 'mp'), parts along dimension 0, may hold values from -6 to 6
- adapter_down: bfloat16 [32, 8192, 64], P(('groups', 'dp', 'mp')), parts along dimension 0, may hold values from -0.0625 to 0.0625
- adapter_up: bfloat16 [32, 64, 1024], P(('groups', 'dp', 'mp')), parts along dimension 0, may hold values from -0.75 to 0.75
- seg_tiles: int32 [4, 24], P(('groups', 'dp')), parts along dimension 0, may hold values from 1 to 4, 32 in all within a row
- seg_adapter: int32 [96, 1], P(('groups', 'dp')), parts along dimension 0, may hold values from 0 to 15
- owner_slot: int32 [32], P('groups'), parts along dimension 0, may hold values from 0 to 15, each once
Outputs:
- output: bfloat16 [16384, 1024], P(('groups', 'dp'), 'mp'), parts along dimension 0
- token_gradient: bfloat16 [16384, 8192], P(('groups', 'dp'), 'mp'), parts along dimension 0
- down_gradient: float32 [32, 8192, 64], P(('groups', 'dp', 'mp')), parts along dimension 0
- up_gradient: float32 [32, 64, 1024], P(('groups', 'dp', 'mp')), parts along dimension 0
The draws below stay inside these ranges and needn't reach their ends.
There are 2 independent parts, one for each index of `groups`. The reference program is written for one: setup_inputs(seed, part) draws one part's arguments, and reference() takes and returns one part's arrays. A program takes and returns all parts, laid end to end along the dimension named above; an argument that names none is the same for every part. Nothing has to cross between parts.
Inputs may be any that keep to these rules, and one draw needn't show every extreme that they name: `seg_tiles`: each row sums to 32; some segment has exactly 4 tiles. `seg_adapter`: every adapter is named by some segment. `owner_slot`: A permutation: each slot holds one adapter.
All inputs are finite; a program needn't handle non-finite values.
Results may differ from the reference program's by a relative error of at most 0.001.
Values may be sent and summed in bfloat16 or wider, within the bound.
No kernel may reach another device: no remote copies, remote signals or barrier semaphores. Data moves between devices by JAX's collectives and lax.ppermute only.
A program may use at most 192 MiB of HBM per device.

```python
import math
import jax
import jax.numpy as jnp
import numpy as np
from jax import lax

MODEL_WIDTH = 8192
OUTW = 1024
RANK = 64
TILE = 128
SEG_MOST = 4
TOK_DEV = 4096
TILE_DEV = 32
SEG_DEV = 24
ADAPTER_COUNT = 16
TOKENS = 8192
N_DP = 2


def strengthened(drawn, rng, source, target, shards_of, factor):
    def block_of(axis_at):
        return (jnp.arange(drawn.shape[axis_at]) // (drawn.shape[axis_at] // shards_of)).reshape((-1,) + (1,) * (drawn.ndim - 1 - axis_at))

    near = jax.random.permutation(rng, shards_of)[block_of(target)]
    far = (block_of(target) + shards_of // 2) % shards_of
    return jnp.where((block_of(source) == near) | (block_of(source) == far), factor * drawn, drawn)


def block_scale(key, dims, split, least, largest):
    level, own = 1.0, jax.random.fold_in(key, 6)
    for position, parts in split:
        draws = jnp.exp(jax.random.uniform(jax.random.fold_in(own, position), (parts,), jnp.float32, least / len(split), largest / len(split)))
        level = level * jnp.repeat(draws, dims[position] // parts).reshape([-1 if axis == position else 1 for axis in range(len(dims))])
    return level


def picks_of(own_key, rows, count, top, lift):
    ranking = jax.random.permutation(jax.random.fold_in(own_key, 1), count)
    boost = ranking
    for power in range(3):
        boost = boost * boost // count
    boost = boost * lift // count
    chance = jax.random.randint(jax.random.fold_in(own_key, 2), (rows, count), 0, 4096) + boost
    holders = jax.random.permutation(jax.random.fold_in(own_key, 3), rows)[jnp.arange(count) % rows]
    chance = jnp.where(jnp.arange(rows)[:, None] == holders[None, :], 1 << 14, chance)
    score = chance * count + jnp.arange(count)
    return lax.top_k(score.astype(jnp.int32), top)[1].astype(jnp.int32)


def split_up(number_of, total, limit, lean):
    loads = [(1 << 20) // math.isqrt(rank ** lean) + 1 for rank in range(2, number_of + 1)]
    spare, counts = total - limit - (number_of - 1), [1] * (number_of - 1)
    while spare > 0:
        free = [i for i in range(number_of - 1) if counts[i] < limit]
        whole, left = sum([loads[i] for i in free]), spare
        for i in free:
            addition = min(limit - counts[i], max(1, left * loads[i] // whole), spare)
            counts[i] = counts[i] + addition
            spare = spare - addition
    return np.array([limit] + counts)


def uneven_parts(own_key, amount, total, bound, lean):
    if amount == 2:
        one = jax.random.randint(own_key, (), max(1, total - bound), min(bound, total - 1) + 1)
        return jnp.stack([one, total - one])
    tallies = jnp.asarray(split_up(amount, total, bound, lean), jnp.int32)
    twos = (amount - 1) // 2
    donor, receiver = tallies[1:1 + 2 * twos:2], tallies[2:2 + 2 * twos:2]
    margin = jnp.minimum(donor - 1, bound - receiver)
    passed = jax.random.randint(jax.random.fold_in(own_key, 1), (twos,), 0, 1 << 20) % (margin + 1)
    tallies = tallies.at[1:1 + 2 * twos:2].set(donor - passed).at[2:2 + 2 * twos:2].set(receiver + passed)
    return tallies[jax.random.permutation(jax.random.fold_in(own_key, 2), amount)]


def centred(stream_key, extent, spread, reach, cuts=(), kind=jnp.bfloat16):
    result = jax.random.normal(stream_key, extent, jnp.float32) * spread
    if len(cuts) > 0:
        result = block_scale(stream_key, extent, cuts, -0.22, 0.18) * result
    return jnp.clip(result, min=-reach, max=reach).astype(kind)


def gaussian_with(rng, shape, spread, bound, cuts, heavy, held_as=jnp.bfloat16):
    drawn = spread * jax.random.normal(rng, shape, jnp.float32)
    if cuts:
        drawn = drawn * block_scale(rng, shape, cuts, -0.22, 0.18)
    return jnp.clip(strengthened(drawn, jax.random.fold_in(rng, 3), *heavy), -bound, bound).astype(held_as)


def setup_inputs(seed: int = 0, part: int = 0) -> dict:
    key_of = jax.random.split(jax.random.key(seed), 9)
    part_splits = jax.random.split(jax.random.fold_in(key_of[8], part), 9)
    tokens = centred(part_splits[0], (TOKENS, MODEL_WIDTH), 1.0, 6.0, ((0, 2), (1, 8)))
    frozen_weight = gaussian_with(key_of[1], (MODEL_WIDTH, OUTW), MODEL_WIDTH ** -0.5, 0.09375, ((0, 8),), (0, 1, 8, 2.0))
    cotangent = centred(part_splits[2], (TOKENS, OUTW), 1.0, 6.0, ((0, 2), (1, 8)))
    adapter_down = centred(part_splits[3], (ADAPTER_COUNT, MODEL_WIDTH, RANK), MODEL_WIDTH ** -0.5, 0.0625, ((0, 16),))
    adapter_up = centred(part_splits[4], (ADAPTER_COUNT, RANK, OUTW), RANK ** -0.5, 0.75, ((0, 16),))
    seg_tiles = jax.vmap(lambda own: uneven_parts(own, SEG_DEV, TILE_DEV, SEG_MOST, 2))(jax.random.split(part_splits[5], N_DP)).reshape((N_DP, SEG_DEV)).astype(jnp.int32)
    seg_adapter = picks_of(part_splits[6], (N_DP * SEG_DEV), ADAPTER_COUNT, 1, 512)
    owner_slot = jax.random.permutation(part_splits[7], ADAPTER_COUNT).astype(jnp.int32)
    return dict(tokens=tokens, frozen_weight=frozen_weight, cotangent=cotangent, adapter_down=adapter_down, adapter_up=adapter_up, seg_tiles=seg_tiles, seg_adapter=seg_adapter, owner_slot=owner_slot)


ADAPTER_SCALE = 2.0
HIGH_ACCURACY = lax.Precision.HIGHEST


def reference(tokens, frozen_weight, cotangent, adapter_down, adapter_up, seg_tiles, seg_adapter, owner_slot):
    token_everything = tokens.shape[0]
    tile_all = token_everything // TILE
    per_block = TOK_DEV // TILE
    seg_table = seg_adapter.reshape(N_DP, SEG_DEV)
    ends = jnp.cumsum(seg_tiles, axis=1).astype(jnp.int32)
    positions = jnp.arange(per_block, dtype=jnp.int32)
    segment = jnp.sum((positions[None, :, None] >= ends[:, None, :]).astype(jnp.int32), axis=2).astype(jnp.int32)
    tile_adapter = jnp.take_along_axis(seg_table, segment, axis=1).reshape(tile_all).astype(jnp.int32)
    tile_slot_index = owner_slot[tile_adapter].astype(jnp.int32)
    down_weight_tiles = adapter_down[tile_slot_index].astype(jnp.float32)
    up_tiles = adapter_up[tile_slot_index].astype(jnp.float32)
    x_tiles = tokens.reshape(tile_all, TILE, MODEL_WIDTH).astype(jnp.float32)
    g_tiles = cotangent.reshape(tile_all, TILE, OUTW).astype(jnp.float32)
    shrink = jnp.einsum("tkd,tdr->tkr", x_tiles, down_weight_tiles, precision=HIGH_ACCURACY)
    base_output = jnp.dot(tokens, frozen_weight, preferred_element_type=jnp.float32)
    raised_rows = jnp.einsum("tkr,tro->tko", shrink, up_tiles, precision=HIGH_ACCURACY).reshape(token_everything, OUTW)
    output = (base_output + ADAPTER_SCALE * raised_rows).astype(jnp.bfloat16)
    backward_result = jnp.einsum("tko,tro->tkr", g_tiles, up_tiles, precision=HIGH_ACCURACY)
    base_gradient = jnp.dot(cotangent, frozen_weight.T, preferred_element_type=jnp.float32)
    adapter_gradient = jnp.einsum("lcu,lwu->lcw", backward_result, down_weight_tiles, precision=HIGH_ACCURACY).reshape(token_everything, MODEL_WIDTH)
    token_gradient = (base_gradient + ADAPTER_SCALE * adapter_gradient).astype(jnp.bfloat16)
    tile_down_weight = jnp.einsum("tkd,tkr->tdr", x_tiles, backward_result, precision=HIGH_ACCURACY)
    tile_up_weight = jnp.einsum("tkr,tko->tro", shrink, g_tiles, precision=HIGH_ACCURACY)
    down_gradient = ADAPTER_SCALE * jax.ops.segment_sum(tile_down_weight, tile_slot_index, num_segments=ADAPTER_COUNT)
    up_gradient = ADAPTER_SCALE * jax.ops.segment_sum(tile_up_weight, tile_slot_index, num_segments=ADAPTER_COUNT)
    return output, token_gradient, down_gradient, up_gradient
```

```python
import functools

import jax
import jax.numpy as jnp
from jax import lax
from jax.experimental import pallas as pl
from jax.experimental.pallas import tpu as pltpu
from jax.sharding import PartitionSpec as P

TILE = 128
ADAPTER_SCALE = 2.0
INNER = 2
PAD = 16
TOP = 32700.0
STEPS = 64.0
TINY = 1e-30
VMEM = 60 * 1024 * 1024
F32 = jnp.float32
BF16 = jnp.bfloat16
NT = (((1,), (1,)), ((), ()))
TN = (((0,), (0,)), ((), ()))


def dot(a, b, dims=(((1,), (0,)), ((), ()))):
    return lax.dot_general(a, b, dims, preferred_element_type=F32)


def split_halves(twice, rank):
    high = twice.astype(BF16).astype(F32)
    lane = lax.broadcasted_iota(jnp.int32, twice.shape, 1)
    return jnp.where(lane < rank, high, twice - high).astype(BF16)


def encode(v):
    most = jnp.max(jnp.abs(v), axis=0, keepdims=True)
    code = jnp.ceil(jnp.log2(jnp.maximum(most, TINY)) * STEPS)
    gain = jnp.exp2(code * (-1.0 / STEPS)) * TOP
    return jnp.round(v * gain).astype(jnp.int32).astype(jnp.int16), code


def step_of(code):
    return jnp.exp2(code.astype(jnp.int32).astype(F32) * (1.0 / STEPS)) * (1.0 / TOP)


def decode(q, code):
    return q.astype(jnp.int32).astype(F32) * step_of(code)


def turn_kernel(in_ref, out_ref):
    out_ref[0] = in_ref[0].T


def forward_kernel(slot_ref, x_ref, w_ref, down_ref, up_ref, part_ref, split_ref):
    step = pl.program_id(0)
    n, rows, cols = part_ref.shape
    tiles = rows // TILE
    rank = down_ref.shape[1] // 2
    base = dot(x_ref[...], w_ref[...])
    for t in range(tiles):
        at = slice(t * TILE, (t + 1) * TILE)
        slot = slot_ref[step * tiles + t]
        pieces = split_halves(dot(x_ref[at, :], down_ref[slot], NT), rank)
        split_ref[at, :] = pieces
        total = base[at] + ADAPTER_SCALE * dot(pieces, up_ref[slot])
        for j in range(n):
            part_ref[j, at, :] = total[:, j * cols : (j + 1) * cols]


def backward_kernel(blocks, slot_ref, place_ref, *refs):
    cots = refs[:blocks]
    x_ref, w_ref, down_ref, up_ref, split_ref, tg_ref, gdown_ref, gup_ref, cot_ref = refs[blocks:]
    step = pl.program_id(0)
    rows = x_ref.shape[0]
    tiles = rows // TILE
    rank = down_ref.shape[1] // 2

    @pl.when(step == 0)
    def _():
        gdown_ref[...] = jnp.zeros_like(gdown_ref)
        gup_ref[...] = jnp.zeros_like(gup_ref)

    if blocks == 1:
        cot_ref[...] = cots[0][...]
    else:
        for j, block in enumerate(cots):
            wide = block.shape[1]
            cot_ref[:, pl.ds(pl.multiple_of(place_ref[j] * wide, wide), wide)] = block[...]
    base = dot(cot_ref[...], w_ref[...], NT)
    for t in range(tiles):
        at = slice(t * TILE, (t + 1) * TILE)
        slot = slot_ref[step * tiles + t]
        cot = cot_ref[at, :]
        pieces = split_halves(dot(cot, up_ref[slot], NT), rank)
        tg_ref[at, :] = (base[at] + ADAPTER_SCALE * dot(pieces, down_ref[slot])).astype(BF16)
        grad = dot(pieces, x_ref[at, :], TN)
        gdown_ref[slot] += grad[:rank] + grad[rank:]
        grad = dot(split_ref[at, :], cot, TN)
        gup_ref[slot] += grad[:rank] + grad[rank:]


def sum_kernel(coded, block_rows, pick_ref, *refs):
    total = refs[0][0]
    for ref in refs[1 : 1 + coded]:
        total = total + decode(ref[0, 0, :block_rows, :], ref[0, 0, block_rows : block_rows + 1, :])
    out_ref = refs[-1]
    if out_ref.dtype == BF16:
        out_ref[...] = total.astype(BF16)
    else:
        q, code = encode(total)
        out_ref[0, 0, :block_rows, :] = q
        out_ref[0, 0, block_rows:, :] = jnp.broadcast_to(code, (PAD, code.shape[1])).astype(jnp.int32).astype(jnp.int16)


def add_parts(part, part_picks, coded, coded_picks, first, blocks, block_rows, last):
    n, rows, cols = part.shape
    count = len(part_picks)
    picks = jnp.stack([jnp.stack([jnp.asarray(i, jnp.int32) for i in p]) for p in (part_picks, *coded_picks)])

    def spec(k):
        return pl.BlockSpec((1, 1, block_rows + PAD, cols), lambda i, b, pick: (pick[k, i], b, 0, 0))

    in_specs = [pl.BlockSpec((1, block_rows, cols), lambda i, b, pick: (pick[0, i], first + b, 0))]
    in_specs += [spec(k + 1) for k in range(len(coded))]
    if last:
        out_shape = jax.ShapeDtypeStruct((blocks * block_rows, cols), BF16)
        out_spec = pl.BlockSpec((block_rows, cols), lambda i, b, pick: (b, 0))
    else:
        out_shape = jax.ShapeDtypeStruct((count, blocks, block_rows + PAD, cols), jnp.int16)
        out_spec = pl.BlockSpec((1, 1, block_rows + PAD, cols), lambda i, b, pick: (i, b, 0, 0))
    values = count * blocks * block_rows * cols
    return pl.pallas_call(
        functools.partial(sum_kernel, len(coded), block_rows),
        grid_spec=pltpu.PrefetchScalarGridSpec(
            num_scalar_prefetch=1, grid=(count, blocks), in_specs=in_specs, out_specs=out_spec
        ),
        out_shape=out_shape,
        cost_estimate=pl.CostEstimate(flops=0, bytes_accessed=values * (6 + 2 * len(coded)), transcendentals=0),
        name="add_parts",
    )(picks, part, *coded)


def pack_kernel(gdown_ref, rdown_ref, gup_ref, rup_ref, out_ref):
    rank, width = gdown_ref.shape[1:]
    groups = gup_ref.shape[2] // width
    row = lax.broadcasted_iota(jnp.int32, (PAD, width), 0)
    codes = jnp.zeros((PAD, width), F32)
    down = gdown_ref[0] + rdown_ref[0]
    for g in range(groups + 1):
        if g == 0:
            v = down
        else:
            at = slice((g - 1) * width, g * width)
            v = gup_ref[0, :, at] + rup_ref[0, :, at]
        q, code = encode(v)
        out_ref[0, g * rank : (g + 1) * rank, :] = q
        codes = jnp.where(row == g, code, codes)
    out_ref[0, (groups + 1) * rank :, :] = codes.astype(jnp.int32).astype(jnp.int16)


def unpack_kernel(in_ref, down_ref, up_ref):
    rank = up_ref.shape[1]
    width = in_ref.shape[2]
    groups = up_ref.shape[2] // width

    @pl.when(pl.program_id(0) == 0)
    def _():
        up_ref[...] = jnp.zeros_like(up_ref)

    steps = ADAPTER_SCALE * step_of(in_ref[0, (groups + 1) * rank :, :])
    for g in range(groups + 1):
        v = in_ref[0, g * rank : (g + 1) * rank, :].astype(jnp.int32).astype(F32) * steps[g : g + 1]
        if g == 0:
            down_ref[0] = v.T
        else:
            up_ref[0, :, (g - 1) * width : g * width] += v


def body(
    tokens, frozen_weight, cotangent, adapter_down, adapter_up, seg_tiles, seg_adapter, owner_slot
):
    rows, width = tokens.shape
    cols = cotangent.shape[1]
    n = lax.axis_size("mp")
    n_data = lax.axis_size("dp")
    _, entire_width, rank = adapter_down.shape
    out_width = adapter_up.shape[2]
    slots = n_data * n
    tile_count = rows // TILE
    inner = INNER
    outer = n // inner
    me = lax.axis_index("mp")
    my_outer, my_inner = me // inner, me % inner
    other = 1 - my_inner
    my_data = lax.axis_index("dp")
    swap = [(i, i ^ 1) for i in range(n)]
    ring = [(i, (i + inner) % n) for i in range(n)]
    cores = [(i, 1 - i) for i in range(n_data)]

    cots, places = [], []
    block = cotangent
    for s in range(outer):
        at = ((my_outer - s) % outer) * inner
        cots += [block, lax.ppermute(block, "mp", swap)]
        places += [at + my_inner, at + other]
        if s < outer - 1:
            block = lax.ppermute(block, "mp", ring)

    turned = pl.pallas_call(
        turn_kernel,
        grid=(n,),
        in_specs=[pl.BlockSpec((1, width, rank), lambda i: (0, i, 0))],
        out_specs=pl.BlockSpec((1, rank, width), lambda i: (i, 0, 0)),
        out_shape=jax.ShapeDtypeStruct((n, rank, width), BF16),
        name="turn_down",
    )(adapter_down)
    down = lax.all_to_all(turned, "mp", split_axis=0, concat_axis=0, tiled=True)
    up = lax.all_gather(adapter_up, "mp", axis=0, tiled=True)
    down = jnp.concatenate([down, lax.ppermute(down, "dp", cores)], axis=0)
    up = jnp.concatenate([up, lax.ppermute(up, "dp", cores)], axis=0)
    down = jnp.concatenate([down, down], axis=1)
    up = jnp.concatenate([up, up], axis=1)

    ends = jnp.cumsum(seg_tiles[0])
    positions = jnp.arange(tile_count, dtype=jnp.int32)
    segment = jnp.sum((positions[:, None] >= ends[None, :]).astype(jnp.int32), axis=1)
    seg_pick = segment[:, None] == jnp.arange(ends.shape[0], dtype=jnp.int32)[None, :]
    tile_adapter = jnp.sum(jnp.where(seg_pick, seg_adapter[:, 0][None, :], 0), axis=1)
    adapt_pick = tile_adapter[:, None] == jnp.arange(slots, dtype=jnp.int32)[None, :]
    tile_slot = jnp.sum(jnp.where(adapt_pick, owner_slot[None, :], 0), axis=1)
    tile_slot = ((tile_slot // n + my_data) % n_data) * n + tile_slot % n

    block_rows = 4 * TILE
    steps = rows // block_rows
    once = pl.Buffered(1)
    part, split = pl.pallas_call(
        forward_kernel,
        grid_spec=pltpu.PrefetchScalarGridSpec(
            num_scalar_prefetch=1,
            grid=(steps,),
            in_specs=[
                pl.BlockSpec((block_rows, width), lambda i, s: (i, 0)),
                pl.BlockSpec((width, out_width), lambda i, s: (0, 0), pipeline_mode=once),
                pl.BlockSpec((slots, 2 * rank, width), lambda i, s: (0, 0, 0), pipeline_mode=once),
                pl.BlockSpec((slots, 2 * rank, out_width), lambda i, s: (0, 0, 0), pipeline_mode=once),
            ],
            out_specs=[
                pl.BlockSpec((n, block_rows, cols), lambda i, s: (0, i, 0)),
                pl.BlockSpec((block_rows, 2 * rank), lambda i, s: (i, 0)),
            ],
        ),
        out_shape=[
            jax.ShapeDtypeStruct((n, rows, cols), F32),
            jax.ShapeDtypeStruct((rows, 2 * rank), BF16),
        ],
        compiler_params=pltpu.CompilerParams(vmem_limit_bytes=VMEM),
        cost_estimate=pl.CostEstimate(
            flops=3 * rows * width * out_width, bytes_accessed=rows * (width * 2 + out_width * 4), transcendentals=0
        ),
        name="forward",
    )(tile_slot, tokens, frozen_weight, down, up)

    chunks = 4
    blocks = steps // chunks
    outs = []
    for c in range(chunks):
        add = functools.partial(add_parts, part, first=c * blocks, blocks=blocks, block_rows=block_rows)
        sent = add([z * inner + other for z in range(outer)], [], [], last=False)
        near = lax.ppermute(sent, "mp", swap)
        got, got_picks = [near], []
        for s in range(1, outer + 1):
            z = (my_outer - s) % outer
            coded_picks = [[z]] if s == 1 else [[z], [0]]
            total = add([z * inner + my_inner], got, coded_picks, last=s == outer)
            if s < outer:
                got = [near, lax.ppermute(total, "mp", ring)]
        outs.append(total)
    output = jnp.concatenate(outs, axis=0)

    if cols % 128:
        order = jnp.stack(cots)[jnp.argsort(jnp.stack(places))]
        cots = [jnp.transpose(order, (1, 0, 2)).reshape(rows, out_width)]
    token_gradient, gdown, gup = pl.pallas_call(
        functools.partial(backward_kernel, len(cots)),
        grid_spec=pltpu.PrefetchScalarGridSpec(
            num_scalar_prefetch=2,
            grid=(steps,),
            in_specs=[pl.BlockSpec((block_rows, a.shape[1]), lambda i, s, p: (i, 0)) for a in cots]
            + [
                pl.BlockSpec((block_rows, width), lambda i, s, p: (i, 0)),
                pl.BlockSpec((width, out_width), lambda i, s, p: (0, 0), pipeline_mode=once),
                pl.BlockSpec((slots, 2 * rank, width), lambda i, s, p: (0, 0, 0), pipeline_mode=once),
                pl.BlockSpec((slots, 2 * rank, out_width), lambda i, s, p: (0, 0, 0), pipeline_mode=once),
                pl.BlockSpec((block_rows, 2 * rank), lambda i, s, p: (i, 0)),
            ],
            out_specs=[
                pl.BlockSpec((block_rows, width), lambda i, s, p: (i, 0)),
                pl.BlockSpec((slots, rank, width), lambda i, s, p: (0, 0, 0), pipeline_mode=once),
                pl.BlockSpec((slots, rank, out_width), lambda i, s, p: (0, 0, 0), pipeline_mode=once),
            ],
            scratch_shapes=[pltpu.VMEM((block_rows, out_width), BF16)],
        ),
        out_shape=[
            jax.ShapeDtypeStruct((rows, width), BF16),
            jax.ShapeDtypeStruct((slots, rank, width), F32),
            jax.ShapeDtypeStruct((slots, rank, out_width), F32),
        ],
        compiler_params=pltpu.CompilerParams(vmem_limit_bytes=VMEM),
        cost_estimate=pl.CostEstimate(
            flops=4 * rows * width * out_width, bytes_accessed=rows * (width * 4 + out_width * 2), transcendentals=0
        ),
        name="backward",
    )(tile_slot, jnp.stack(places).astype(jnp.int32), *cots, tokens, frozen_weight, down, up, split)

    rdown = lax.ppermute(gdown[n:], "dp", cores)
    rup = lax.ppermute(gup[n:], "dp", cores)
    packed_rows = (1 + out_width // width) * rank + PAD
    packed = pl.pallas_call(
        pack_kernel,
        grid=(n,),
        in_specs=[
            pl.BlockSpec((1, rank, width), lambda i: (i, 0, 0)),
            pl.BlockSpec((1, rank, width), lambda i: (i, 0, 0)),
            pl.BlockSpec((1, rank, out_width), lambda i: (i, 0, 0)),
            pl.BlockSpec((1, rank, out_width), lambda i: (i, 0, 0)),
        ],
        out_specs=pl.BlockSpec((1, packed_rows, width), lambda i: (i, 0, 0)),
        out_shape=jax.ShapeDtypeStruct((n, packed_rows, width), jnp.int16),
        name="pack_gradients",
    )(gdown, rdown, gup, rup)
    packed = lax.all_to_all(packed, "mp", split_axis=0, concat_axis=0, tiled=True)
    down_gradient, up_gradient = pl.pallas_call(
        unpack_kernel,
        grid=(n,),
        in_specs=[pl.BlockSpec((1, packed_rows, width), lambda i: (i, 0, 0))],
        out_specs=[
            pl.BlockSpec((1, width, rank), lambda i: (0, i, 0)),
            pl.BlockSpec((1, rank, out_width), lambda i: (0, 0, 0)),
        ],
        out_shape=[
            jax.ShapeDtypeStruct((1, entire_width, rank), F32),
            jax.ShapeDtypeStruct((1, rank, out_width), F32),
        ],
        name="unpack_gradients",
    )(packed)
    return output, token_gradient, down_gradient, up_gradient


def solution(mesh):
    placed = (
        P(("groups", "dp"), "mp"),
        P("mp", None),
        P(("groups", "dp"), "mp"),
        P(("groups", "dp", "mp"), None, None),
        P(("groups", "dp", "mp"), None, None),
        P(("groups", "dp"), None),
        P(("groups", "dp"), None),
        P("groups"),
    )
    return jax.shard_map(
        body,
        mesh=mesh,
        in_specs=placed,
        out_specs=(
            P(("groups", "dp"), "mp"),
            P(("groups", "dp"), "mp"),
            P(("groups", "dp", "mp"), None, None),
            P(("groups", "dp", "mp"), None, None),
        ),
        check_vma=False,
    )
```

```python
import functools

import jax
import jax.numpy as jnp
from jax import lax
from jax.experimental import pallas as pl
from jax.experimental.pallas import tpu as pltpu
from jax.sharding import PartitionSpec as P

TILE = 128
ADAPTER_SCALE = 2.0
INNER = 2
PAD = 16
TOP = 32700.0
STEPS = 64.0
TINY = 1e-30
VMEM = 60 * 1024 * 1024
F32 = jnp.float32
BF16 = jnp.bfloat16
NT = (((1,), (1,)), ((), ()))
TN = (((0,), (0,)), ((), ()))


def dot(a, b, dims=(((1,), (0,)), ((), ()))):
    return lax.dot_general(a, b, dims, preferred_element_type=F32)


def split_halves(twice, rank):
    high = twice.astype(BF16).astype(F32)
    lane = lax.broadcasted_iota(jnp.int32, twice.shape, 1)
    return jnp.where(lane < rank, high, twice - high).astype(BF16)


def encode(v):
    most = jnp.max(jnp.abs(v), axis=0, keepdims=True)
    code = jnp.ceil(jnp.log2(jnp.maximum(most, TINY)) * STEPS)
    gain = jnp.exp2(code * (-1.0 / STEPS)) * TOP
    return jnp.round(v * gain).astype(jnp.int32).astype(jnp.int16), code


def step_of(code):
    return jnp.exp2(code.astype(jnp.int32).astype(F32) * (1.0 / STEPS)) * (1.0 / TOP)


def decode(q, code):
    return q.astype(jnp.int32).astype(F32) * step_of(code)


def turn_kernel(in_ref, out_ref):
    out_ref[0] = in_ref[0].T


def fill_twice(pair_ref, near_ref, far_ref):
    n, rank = near_ref.shape[:2]
    for k, ref in enumerate((near_ref, far_ref)):
        pair_ref[k * n : (k + 1) * n, :rank, :] = ref[...]
        pair_ref[k * n : (k + 1) * n, rank:, :] = ref[...]


def forward_kernel(first, slot_ref, upslot_ref, place_ref, *refs):
    x_ref, w_ref, ndown_ref, fdown_ref, nup_ref, fup_ref, sent_ref, kept_ref, split_ref, down_ref, up_ref, sum_ref = refs
    step = pl.program_id(0)
    outer, rows, cols = kept_ref.shape
    tiles = rows // TILE
    rank = down_ref.shape[1] // 2
    n = ndown_ref.shape[0]
    inner = n // outer

    @pl.when(step == 0)
    def _():
        fill_twice(down_ref, ndown_ref, fdown_ref)
        fill_twice(up_ref, nup_ref, fup_ref)

    base = dot(x_ref[...], w_ref[...])
    for t in range(tiles):
        at = slice(t * TILE, (t + 1) * TILE)
        tile = first + step * tiles + t
        pieces = split_halves(dot(x_ref[at, :], down_ref[slot_ref[tile]], NT), rank)
        split_ref[at, :] = pieces
        total = base[at] + ADAPTER_SCALE * dot(pieces, up_ref[upslot_ref[tile]])
        for j in range(n):
            sum_ref[j, at, :] = total[:, j * cols : (j + 1) * cols]
    mine = place_ref[1]
    for z in range(outer):
        kept_ref[z] = sum_ref[z * inner + mine]
        q, code = encode(sum_ref[z * inner + 1 - mine])
        put(sent_ref.at[z, 0], q, code)


def gradient_kernel(blocks, slot_ref, upslot_ref, order_ref, *refs):
    cots = refs[:blocks]
    x_ref, nup_ref, fup_ref, split_ref = refs[blocks : blocks + 4]
    all_ref, back_ref, ndown_ref, fdown_ref, nsum_ref, fsum_ref, up_ref, cot_ref, gdown_ref, gup_ref = refs[blocks + 4 :]
    step = pl.program_id(0)
    rows = x_ref.shape[0]
    tiles = rows // TILE
    rank = up_ref.shape[1] // 2

    @pl.when(step == 0)
    def _():
        fill_twice(up_ref, nup_ref, fup_ref)
        gdown_ref[...] = jnp.zeros_like(gdown_ref)
        gup_ref[...] = jnp.zeros_like(gup_ref)

    for j, block in enumerate(cots):
        wide = block.shape[1]
        if blocks == 1:
            cot_ref[...] = block[...]
        else:
            cot_ref[:, pl.ds(pl.multiple_of(order_ref[j] * wide, wide), wide)] = block[...]
    all_ref[...] = cot_ref[...]
    for t in range(tiles):
        at = slice(t * TILE, (t + 1) * TILE)
        slot = slot_ref[step * tiles + t]
        cot = cot_ref[at, :]
        pieces = split_halves(dot(cot, up_ref[upslot_ref[step * tiles + t]], NT), rank)
        back_ref[at, :] = pieces
        grad = dot(pieces, x_ref[at, :], TN)
        gdown_ref[slot] += grad[:rank] + grad[rank:]
        grad = dot(split_ref[at, :], cot, TN)
        gup_ref[slot] += grad[:rank] + grad[rank:]

    @pl.when(step == pl.num_programs(0) - 1)
    def _():
        n = ndown_ref.shape[0]
        ndown_ref[...] = gdown_ref[:n]
        fdown_ref[...] = gdown_ref[n:]
        nsum_ref[...] = gup_ref[:n]
        fsum_ref[...] = gup_ref[n:]


def token_kernel(slot_ref, cot_ref, w_ref, near_ref, far_ref, back_ref, after_ref, out_ref, down_ref):
    step = pl.program_id(0)
    tiles = cot_ref.shape[0] // TILE

    @pl.when(step == 0)
    def _():
        fill_twice(down_ref, near_ref, far_ref)

    base = dot(cot_ref[...], w_ref[...], NT)
    for t in range(tiles):
        at = slice(t * TILE, (t + 1) * TILE)
        slot = slot_ref[step * tiles + t]
        out_ref[at, :] = (base[at] + ADAPTER_SCALE * dot(back_ref[at, :], down_ref[slot])).astype(BF16)


def put(ref, q, code):
    rows = q.shape[0]
    ref[:rows, :] = q
    ref[rows:, :] = jnp.broadcast_to(code, (PAD, code.shape[1])).astype(jnp.int32).astype(jnp.int16)


def sum_kernel(coded, place_ref, *refs):
    total = refs[0][0]
    rows = total.shape[0]
    for ref in refs[1 : 1 + coded]:
        total = total + decode(ref[0, 0, :rows, :], ref[0, 0, rows : rows + 1, :])
    out_ref = refs[-1]
    if out_ref.dtype == BF16:
        out_ref[...] = total.astype(BF16)
    else:
        put(out_ref.at[0, 0], *encode(total))


def add_parts(place, back, kept, near, run, last):
    outer, rows, cols = kept.shape
    blocks, held = near.shape[1:3]
    block_rows = held - PAD

    def at(place):
        return lax.rem(place[0] - back + outer, outer)

    in_specs = [
        pl.BlockSpec((1, block_rows, cols), lambda b, p: (at(p), b, 0)),
        pl.BlockSpec((1, 1, held, cols), lambda b, p: (at(p), b, 0, 0)),
    ]
    in_specs += [pl.BlockSpec((1, 1, held, cols), lambda b, p: (0, b, 0, 0)) for _ in run]
    if last:
        out_shape = jax.ShapeDtypeStruct((rows, cols), BF16)
        out_spec = pl.BlockSpec((block_rows, cols), lambda b, p: (b, 0))
    else:
        out_shape = jax.ShapeDtypeStruct((1, blocks, held, cols), jnp.int16)
        out_spec = pl.BlockSpec((1, 1, held, cols), lambda b, p: (0, b, 0, 0))
    return pl.pallas_call(
        functools.partial(sum_kernel, 1 + len(run)),
        grid_spec=pltpu.PrefetchScalarGridSpec(
            num_scalar_prefetch=1, grid=(blocks,), in_specs=in_specs, out_specs=out_spec
        ),
        out_shape=out_shape,
        cost_estimate=pl.CostEstimate(flops=0, bytes_accessed=rows * cols * 8, transcendentals=0),
        name="add_parts",
    )(place, kept, near, *run)


def pack_kernel(gdown_ref, rdown_ref, gup_ref, rup_ref, out_ref):
    rank, width = gdown_ref.shape[1:]
    groups = gup_ref.shape[2] // width
    row = lax.broadcasted_iota(jnp.int32, (PAD, width), 0)
    codes = jnp.zeros((PAD, width), F32)
    down = gdown_ref[0] + rdown_ref[0]
    for g in range(groups + 1):
        if g == 0:
            v = down
        else:
            at = slice((g - 1) * width, g * width)
            v = gup_ref[0, :, at] + rup_ref[0, :, at]
        q, code = encode(v)
        out_ref[0, g * rank : (g + 1) * rank, :] = q
        codes = jnp.where(row == g, code, codes)
    out_ref[0, (groups + 1) * rank :, :] = codes.astype(jnp.int32).astype(jnp.int16)


def unpack_kernel(in_ref, down_ref, up_ref):
    rank = up_ref.shape[1]
    width = in_ref.shape[2]
    groups = up_ref.shape[2] // width

    @pl.when(pl.program_id(0) == 0)
    def _():
        up_ref[...] = jnp.zeros_like(up_ref)

    steps = ADAPTER_SCALE * step_of(in_ref[0, (groups + 1) * rank :, :])
    for g in range(groups + 1):
        v = in_ref[0, g * rank : (g + 1) * rank, :].astype(jnp.int32).astype(F32) * steps[g : g + 1]
        if g == 0:
            down_ref[0] = v.T
        else:
            up_ref[0, :, (g - 1) * width : g * width] += v


def body(
    tokens, frozen_weight, cotangent, adapter_down, adapter_up, seg_tiles, seg_adapter, owner_slot
):
    rows, width = tokens.shape
    cols = cotangent.shape[1]
    n = lax.axis_size("mp")
    n_data = lax.axis_size("dp")
    _, entire_width, rank = adapter_down.shape
    out_width = adapter_up.shape[2]
    slots = n_data * n
    tile_count = rows // TILE
    inner = INNER
    outer = n // inner
    me = lax.axis_index("mp")
    my_outer, my_inner = me // inner, me % inner
    other = 1 - my_inner
    my_data = lax.axis_index("dp")
    swap = [(i, i ^ 1) for i in range(n)]
    ring = [(i, (i + inner) % n) for i in range(n)]
    cores = [(i, 1 - i) for i in range(n_data)]

    place = jnp.stack([my_outer, my_inner]).astype(jnp.int32)

    ups = [adapter_up]
    for s in range(1, outer):
        ups.append(lax.ppermute(adapter_up, "mp", [(i, (i + s * inner) % n) for i in range(n)]))
    ups = jnp.concatenate(ups, axis=0)
    near_up = jnp.concatenate([ups, lax.ppermute(ups, "mp", swap)], axis=0)
    far_up = lax.ppermute(near_up, "dp", cores)

    turned = pl.pallas_call(
        turn_kernel,
        grid=(n,),
        in_specs=[pl.BlockSpec((1, width, rank), lambda i: (0, i, 0))],
        out_specs=pl.BlockSpec((1, rank, width), lambda i: (i, 0, 0)),
        out_shape=jax.ShapeDtypeStruct((n, rank, width), BF16),
        name="turn_down",
    )(adapter_down)
    near_down = lax.all_to_all(turned, "mp", split_axis=0, concat_axis=0, tiled=True)
    far_down = lax.ppermute(near_down, "dp", cores)

    cots, order = [], []
    block, swapped = cotangent, None
    for s in range(outer):
        at = ((my_outer - s) % outer) * inner
        swapped = lax.ppermute(block, "mp", swap)
        cots += [block, swapped]
        order += [at + my_inner, at + other]
        if s < outer - 1:
            block, cots[-1] = lax.optimization_barrier((lax.ppermute(block, "mp", ring), swapped))

    ends = jnp.cumsum(seg_tiles[0])
    positions = jnp.arange(tile_count, dtype=jnp.int32)
    segment = jnp.sum((positions[:, None] >= ends[None, :]).astype(jnp.int32), axis=1)
    seg_pick = segment[:, None] == jnp.arange(ends.shape[0], dtype=jnp.int32)[None, :]
    tile_adapter = jnp.sum(jnp.where(seg_pick, seg_adapter[:, 0][None, :], 0), axis=1)
    adapt_pick = tile_adapter[:, None] == jnp.arange(slots, dtype=jnp.int32)[None, :]
    tile_slot = jnp.sum(jnp.where(adapt_pick, owner_slot[None, :], 0), axis=1)
    core, owner = (tile_slot // n + my_data) % n_data, tile_slot % n
    tile_slot = core * n + owner
    tile_up = core * n + ((owner + my_inner) % inner) * outer + (my_outer - owner // inner) % outer

    block_rows = 4 * TILE
    steps = rows // block_rows
    chunks = 4
    blocks = steps // chunks
    chunk_rows = rows // chunks
    once = pl.Buffered(1)
    params = pltpu.CompilerParams(vmem_limit_bytes=VMEM)
    held = block_rows + PAD

    def whole(*shape):
        return pl.BlockSpec(shape, lambda i, *_: (0,) * len(shape), pipeline_mode=once)

    def strip(wide, first=0):
        return pl.BlockSpec((block_rows, wide), lambda i, *_: (first + i, 0))

    def forward(c):
        return pl.pallas_call(
            functools.partial(forward_kernel, c * blocks * (block_rows // TILE)),
            grid_spec=pltpu.PrefetchScalarGridSpec(
                num_scalar_prefetch=3,
                grid=(blocks,),
                in_specs=[
                    strip(width, c * blocks),
                    whole(width, out_width),
                    whole(n, rank, width),
                    whole(n, rank, width),
                    whole(n, rank, out_width),
                    whole(n, rank, out_width),
                ],
                out_specs=[
                    pl.BlockSpec((outer, 1, held, cols), lambda i, *_: (0, i, 0, 0)),
                    pl.BlockSpec((outer, block_rows, cols), lambda i, *_: (0, i, 0)),
                    strip(2 * rank),
                ],
                scratch_shapes=[
                    pltpu.VMEM((slots, 2 * rank, width), BF16),
                    pltpu.VMEM((slots, 2 * rank, out_width), BF16),
                    pltpu.VMEM((n, block_rows, cols), F32),
                ],
            ),
            out_shape=[
                jax.ShapeDtypeStruct((outer, blocks, held, cols), jnp.int16),
                jax.ShapeDtypeStruct((outer, chunk_rows, cols), F32),
                jax.ShapeDtypeStruct((chunk_rows, 2 * rank), BF16),
            ],
            compiler_params=params,
            cost_estimate=pl.CostEstimate(
                flops=4 * chunk_rows * width * out_width, bytes_accessed=chunk_rows * width * 6, transcendentals=0
            ),
            name="forward",
        )(tile_slot, tile_up, place, tokens, frozen_weight, near_down, far_down, near_up, far_up)

    sents, kepts, splits = zip(*[forward(c) for c in range(chunks)])
    split = jnp.concatenate(splits, axis=0)
    first, cots[-1] = lax.optimization_barrier((sents[0], cots[-1]))
    nears = [lax.ppermute(first, "mp", swap)]
    for c in range(1, chunks):
        sent, nears[-1] = lax.optimization_barrier((sents[c], nears[-1]))
        nears.append(lax.ppermute(sent, "mp", swap))

    if cols % 128:
        natural = jnp.stack(cots)[jnp.argsort(jnp.stack(order))]
        cots = [jnp.transpose(natural, (1, 0, 2)).reshape(rows, out_width)]
    cot_all, back, gdown, rdown, gup, rup = pl.pallas_call(
        functools.partial(gradient_kernel, len(cots)),
        grid_spec=pltpu.PrefetchScalarGridSpec(
            num_scalar_prefetch=3,
            grid=(steps,),
            in_specs=[strip(a.shape[1]) for a in cots]
            + [strip(width), whole(n, rank, out_width), whole(n, rank, out_width), strip(2 * rank)],
            out_specs=[
                strip(out_width),
                strip(2 * rank),
                whole(n, rank, width),
                whole(n, rank, width),
                whole(n, rank, out_width),
                whole(n, rank, out_width),
            ],
            scratch_shapes=[
                pltpu.VMEM((slots, 2 * rank, out_width), BF16),
                pltpu.VMEM((block_rows, out_width), BF16),
                pltpu.VMEM((slots, rank, width), F32),
                pltpu.VMEM((slots, rank, out_width), F32),
            ],
        ),
        out_shape=[
            jax.ShapeDtypeStruct((rows, out_width), BF16),
            jax.ShapeDtypeStruct((rows, 2 * rank), BF16),
            jax.ShapeDtypeStruct((n, rank, width), F32),
            jax.ShapeDtypeStruct((n, rank, width), F32),
            jax.ShapeDtypeStruct((n, rank, out_width), F32),
            jax.ShapeDtypeStruct((n, rank, out_width), F32),
        ],
        compiler_params=params,
        cost_estimate=pl.CostEstimate(
            flops=2 * rows * width * out_width, bytes_accessed=rows * (width * 2 + out_width * 4), transcendentals=0
        ),
        name="gradients",
    )(tile_slot, tile_up, jnp.stack(order).astype(jnp.int32), *cots, tokens, near_up, far_up, split)
    nears[0], rdown, rup = lax.optimization_barrier((nears[0], rdown, rup))

    outs = []
    for near, kept in zip(nears, kepts):
        run = []
        for s in range(1, outer):
            run = [lax.ppermute(add_parts(place, s, kept, near, run, last=False), "mp", ring)]
        outs.append(add_parts(place, 0, kept, near, run, last=True))
    output = jnp.concatenate(outs, axis=0)

    token_gradient = pl.pallas_call(
        token_kernel,
        grid_spec=pltpu.PrefetchScalarGridSpec(
            num_scalar_prefetch=1,
            grid=(steps,),
            in_specs=[
                strip(out_width),
                whole(width, out_width),
                whole(n, rank, width),
                whole(n, rank, width),
                strip(2 * rank),
                pl.BlockSpec(memory_space=pl.ANY),
            ],
            out_specs=strip(width),
            scratch_shapes=[pltpu.VMEM((slots, 2 * rank, width), BF16)],
        ),
        out_shape=jax.ShapeDtypeStruct((rows, width), BF16),
        compiler_params=params,
        cost_estimate=pl.CostEstimate(
            flops=3 * rows * width * out_width, bytes_accessed=rows * (width * 2 + out_width * 2), transcendentals=0
        ),
        name="token_gradient",
    )(tile_slot, cot_all, frozen_weight, near_down, far_down, back, nears[-1])

    rdown = lax.ppermute(rdown, "dp", cores)
    rup = lax.ppermute(rup, "dp", cores)
    packed_rows = (1 + out_width // width) * rank + PAD
    packed = pl.pallas_call(
        pack_kernel,
        grid=(n,),
        in_specs=[
            pl.BlockSpec((1, rank, width), lambda i: (i, 0, 0)),
            pl.BlockSpec((1, rank, width), lambda i: (i, 0, 0)),
            pl.BlockSpec((1, rank, out_width), lambda i: (i, 0, 0)),
            pl.BlockSpec((1, rank, out_width), lambda i: (i, 0, 0)),
        ],
        out_specs=pl.BlockSpec((1, packed_rows, width), lambda i: (i, 0, 0)),
        out_shape=jax.ShapeDtypeStruct((n, packed_rows, width), jnp.int16),
        name="pack_gradients",
    )(gdown, rdown, gup, rup)
    packed = lax.all_to_all(packed, "mp", split_axis=0, concat_axis=0, tiled=True)
    down_gradient, up_gradient = pl.pallas_call(
        unpack_kernel,
        grid=(n,),
        in_specs=[pl.BlockSpec((1, packed_rows, width), lambda i: (i, 0, 0))],
        out_specs=[
            pl.BlockSpec((1, width, rank), lambda i: (0, i, 0)),
            pl.BlockSpec((1, rank, out_width), lambda i: (0, 0, 0)),
        ],
        out_shape=[
            jax.ShapeDtypeStruct((1, entire_width, rank), F32),
            jax.ShapeDtypeStruct((1, rank, out_width), F32),
        ],
        name="unpack_gradients",
    )(packed)
    return output, token_gradient, down_gradient, up_gradient


def solution(mesh):
    placed = (
        P(("groups", "dp"), "mp"),
        P("mp", None),
        P(("groups", "dp"), "mp"),
        P(("groups", "dp", "mp"), None, None),
        P(("groups", "dp", "mp"), None, None),
        P(("groups", "dp"), None),
        P(("groups", "dp"), None),
        P("groups"),
    )
    return jax.shard_map(
        body,
        mesh=mesh,
        in_specs=placed,
        out_specs=(
            P(("groups", "dp"), "mp"),
            P(("groups", "dp"), "mp"),
            P(("groups", "dp", "mp"), None, None),
            P(("groups", "dp", "mp"), None, None),
        ),
        check_vma=False,
    )
```

```python
import functools

import jax
import jax.numpy as jnp
from jax import lax
from jax.experimental import pallas as pl
from jax.experimental.pallas import tpu as pltpu
from jax.sharding import PartitionSpec as P

TILE = 128
ADAPTER_SCALE = 2.0
INNER = 2
PAD = 16
TOP = 32700.0
STEPS = 64.0
TINY = 1e-30
VMEM = 60 * 1024 * 1024
F32 = jnp.float32
BF16 = jnp.bfloat16
NT = (((1,), (1,)), ((), ()))
TN = (((0,), (0,)), ((), ()))


def dot(a, b, dims=(((1,), (0,)), ((), ()))):
    return lax.dot_general(a, b, dims, preferred_element_type=F32)


def split_halves(twice, rank):
    high = twice.astype(BF16).astype(F32)
    lane = lax.broadcasted_iota(jnp.int32, twice.shape, 1)
    return jnp.where(lane < rank, high, twice - high).astype(BF16)


def encode(v):
    most = jnp.max(jnp.abs(v), axis=0, keepdims=True)
    code = jnp.ceil(jnp.log2(jnp.maximum(most, TINY)) * STEPS)
    gain = jnp.exp2(code * (-1.0 / STEPS)) * TOP
    return jnp.round(v * gain).astype(jnp.int32).astype(jnp.int16), code


def step_of(code):
    return jnp.exp2(code.astype(jnp.int32).astype(F32) * (1.0 / STEPS)) * (1.0 / TOP)


def decode(q, code):
    return q.astype(jnp.int32).astype(F32) * step_of(code)


def copy_kernel(in_ref, out_ref):
    out_ref[...] = in_ref[...]


def fill_twice(pair_ref, near_ref, far_ref):
    n, rank = near_ref.shape[:2]
    for k, ref in enumerate((near_ref, far_ref)):
        pair_ref[k * n : (k + 1) * n, :rank, :] = ref[...]
        pair_ref[k * n : (k + 1) * n, rank:, :] = ref[...]


def shrink_kernel(slot_ref, x_ref, near_ref, far_ref, out_ref, down_ref):
    step = pl.program_id(0)
    n = near_ref.shape[0]

    @pl.when(step == 0)
    def _():
        down_ref[:n] = near_ref[...]
        down_ref[n:] = far_ref[...]

    tiles = x_ref.shape[0] // TILE
    for t in range(tiles):
        at = slice(t * TILE, (t + 1) * TILE)
        out_ref[:, at] = dot(down_ref[slot_ref[step * tiles + t]], x_ref[at, :], NT)


def forward_kernel(first, slot_ref, upslot_ref, place_ref, *refs):
    x_ref, w_ref, ndown_ref, fdown_ref, nup_ref, fup_ref, kept_ref = refs[:7]
    *sent_ref, down_ref, up_ref = refs[7:10] if len(refs) == 11 else refs[7:]
    sum_ref = refs[-1] if sent_ref else kept_ref
    step = pl.program_id(0)
    n, rows, cols = sum_ref.shape
    outer = kept_ref.shape[0]
    inner = n // outer
    tiles = rows // TILE
    rank = down_ref.shape[1] // 2

    @pl.when(step == 0)
    def _():
        fill_twice(down_ref, ndown_ref, fdown_ref)
        fill_twice(up_ref, nup_ref, fup_ref)

    base = dot(x_ref[...], w_ref[...])
    for t in range(tiles):
        at = slice(t * TILE, (t + 1) * TILE)
        tile = first + step * tiles + t
        pieces = split_halves(dot(x_ref[at, :], down_ref[slot_ref[tile]], NT), rank)
        total = base[at] + ADAPTER_SCALE * dot(pieces, up_ref[upslot_ref[tile]])
        for j in range(n):
            sum_ref[j, at, :] = total[:, j * cols : (j + 1) * cols]
    if not sent_ref:
        return
    mine = place_ref[1]
    for z in range(outer):
        kept_ref[z] = sum_ref[z * inner + mine]
        put(sent_ref[0].at[z, 0], *encode(sum_ref[z * inner + 1 - mine]))


def gradient_kernel(blocks, slot_ref, upslot_ref, order_ref, *refs):
    cots = refs[:blocks]
    x_ref, nup_ref, fup_ref, shrink_ref = refs[blocks : blocks + 4]
    all_ref, back_ref, ndown_ref, fdown_ref, nsum_ref, fsum_ref, up_ref, cot_ref, gdown_ref, gup_ref = refs[blocks + 4 :]
    step = pl.program_id(0)
    rows = x_ref.shape[0]
    tiles = rows // TILE
    rank = up_ref.shape[1] // 2

    @pl.when(step == 0)
    def _():
        fill_twice(up_ref, nup_ref, fup_ref)
        gdown_ref[...] = jnp.zeros_like(gdown_ref)
        gup_ref[...] = jnp.zeros_like(gup_ref)

    for j, block in enumerate(cots):
        wide = block.shape[1]
        if blocks == 1:
            cot_ref[...] = block[...]
        else:
            cot_ref[:, pl.ds(pl.multiple_of(order_ref[j] * wide, wide), wide)] = block[...]
    all_ref[...] = cot_ref[...]
    for t in range(tiles):
        at = slice(t * TILE, (t + 1) * TILE)
        tile = step * tiles + t
        slot, cot = slot_ref[tile], cot_ref[at, :]
        pieces = split_halves(dot(cot, up_ref[upslot_ref[tile]], NT), rank)
        back_ref[at, :] = pieces
        grad = dot(pieces, x_ref[at, :], TN)
        gdown_ref[slot] += grad[:rank] + grad[rank:]
        shrink = shrink_ref[:, at]
        high = shrink.astype(BF16)
        low = (shrink - high.astype(F32)).astype(BF16)
        gup_ref[slot] += dot(high, cot) + dot(low, cot)

    @pl.when(step == pl.num_programs(0) - 1)
    def _():
        n = ndown_ref.shape[0]
        ndown_ref[...] = gdown_ref[:n]
        fdown_ref[...] = gdown_ref[n:]
        nsum_ref[...] = gup_ref[:n]
        fsum_ref[...] = gup_ref[n:]


def token_kernel(slot_ref, cot_ref, w_ref, near_ref, far_ref, back_ref, after_ref, out_ref, down_ref):
    step = pl.program_id(0)
    tiles = cot_ref.shape[0] // TILE

    @pl.when(step == 0)
    def _():
        fill_twice(down_ref, near_ref, far_ref)

    base = dot(cot_ref[...], w_ref[...], NT)
    for t in range(tiles):
        at = slice(t * TILE, (t + 1) * TILE)
        slot = slot_ref[step * tiles + t]
        out_ref[at, :] = (base[at] + ADAPTER_SCALE * dot(back_ref[at, :], down_ref[slot])).astype(BF16)


def put(ref, q, code):
    rows = q.shape[0]
    ref[:rows, :] = q
    ref[rows:, :] = jnp.broadcast_to(code, (PAD, code.shape[1])).astype(jnp.int32).astype(jnp.int16)


def sum_kernel(coded, place_ref, *refs):
    total = refs[0][0]
    rows = total.shape[0]
    for ref in refs[1 : 1 + coded]:
        total = total + decode(ref[0, 0, :rows, :], ref[0, 0, rows : rows + 1, :])
    out_ref = refs[-1]
    if out_ref.dtype == BF16:
        out_ref[...] = total.astype(BF16)
    else:
        put(out_ref.at[0, 0], *encode(total))


def add_parts(place, block_rows, count, kept, coded, last=False):
    part, pick = kept
    rows, cols = part.shape[1:]
    blocks, held = rows // block_rows, block_rows + PAD

    def coded_spec(pick):
        return pl.BlockSpec((1, 1, held, cols), lambda i, b, p: (pick(i, p), b, 0, 0))

    in_specs = [pl.BlockSpec((1, block_rows, cols), lambda i, b, p: (pick(i, p), b, 0))]
    in_specs += [coded_spec(q) for _, q in coded]
    if last:
        out_shape = jax.ShapeDtypeStruct((rows, cols), BF16)
        out_spec = pl.BlockSpec((block_rows, cols), lambda i, b, p: (b, 0))
    else:
        out_shape = jax.ShapeDtypeStruct((count, blocks, held, cols), jnp.int16)
        out_spec = coded_spec(lambda i, p: i)
    return pl.pallas_call(
        functools.partial(sum_kernel, len(coded)),
        grid_spec=pltpu.PrefetchScalarGridSpec(
            num_scalar_prefetch=1, grid=(count, blocks), in_specs=in_specs, out_specs=out_spec
        ),
        out_shape=out_shape,
        cost_estimate=pl.CostEstimate(flops=0, bytes_accessed=count * rows * cols * 8, transcendentals=0),
        name="add_parts",
    )(place, part, *[a for a, _ in coded])


def pack_kernel(gdown_ref, rdown_ref, gup_ref, rup_ref, out_ref):
    rank, width = gdown_ref.shape[1:]
    own = gup_ref.shape[1]
    groups = gup_ref.shape[2] // width
    q, code = encode(gdown_ref[0] + rdown_ref[0])
    out_ref[0, :rank, :] = q
    tail, codes = [], [code]
    up = gup_ref[0] + rup_ref[0]
    for g in range(groups):
        q, code = encode(up[:, g * width : (g + 1) * width])
        tail.append(q.astype(jnp.int32))
        codes.append(code)
    row = lax.broadcasted_iota(jnp.int32, (PAD - groups * own, width), 0)
    last = jnp.zeros(row.shape, F32)
    for g, code in enumerate(codes):
        last = jnp.where(row == g, code, last)
    out_ref[0, rank:, :] = jnp.concatenate([*tail, last.astype(jnp.int32)], axis=0).astype(jnp.int16)


def unpack_kernel(in_ref, down_ref, up_ref):
    width = in_ref.shape[2]
    own = up_ref.shape[1]
    groups = up_ref.shape[2] // width
    rank = down_ref.shape[1]
    tail = in_ref[0, rank:, :].astype(jnp.int32).astype(F32)
    steps = jnp.exp2(tail[groups * own :] * (1.0 / STEPS)) * (ADAPTER_SCALE / TOP)
    down_ref[0] = in_ref[0, :rank, :].astype(jnp.int32).astype(F32) * steps[:1]
    for g in range(groups):
        up_ref[0, :, g * width : (g + 1) * width] = tail[g * own : (g + 1) * own] * steps[g + 1 : g + 2]


def body(
    tokens, frozen_weight, cotangent, adapter_down, adapter_up, seg_tiles, seg_adapter, owner_slot
):
    rows, width = tokens.shape
    cols = cotangent.shape[1]
    n = lax.axis_size("mp")
    n_data = lax.axis_size("dp")
    _, entire_width, rank = adapter_down.shape
    out_width = adapter_up.shape[2]
    slots = n_data * n
    tile_count = rows // TILE
    inner = INNER
    outer = n // inner
    me = lax.axis_index("mp")
    my_outer, my_inner = me // inner, me % inner
    other = 1 - my_inner
    my_data = lax.axis_index("dp")
    swap = [(i, i ^ 1) for i in range(n)]
    ring = [(i, (i + inner) % n) for i in range(n)]
    cores = [(i, 1 - i) for i in range(n_data)]

    place = jnp.stack([my_outer, my_inner]).astype(jnp.int32)

    block_rows = 4 * TILE
    steps = rows // block_rows
    sizes = [steps // 4, steps // 4, steps - 2 * (steps // 4)]
    starts = [sum(sizes[:c]) for c in range(len(sizes))]
    chunks = len(sizes)
    once = pl.Buffered(1)
    params = pltpu.CompilerParams(vmem_limit_bytes=VMEM)
    held = block_rows + PAD
    tie = lax.optimization_barrier

    ups = [adapter_up]
    for s in range(1, outer):
        ups.append(lax.ppermute(adapter_up, "mp", [(i, (i + s * inner) % n) for i in range(n)]))
    cut = pl.pallas_call(
        copy_kernel,
        grid=(n,),
        in_specs=[pl.BlockSpec((1, rank, width), lambda i: (0, 0, i))],
        out_specs=pl.BlockSpec((1, rank, width), lambda i: (i, 0, 0)),
        out_shape=jax.ShapeDtypeStruct((n, rank, width), BF16),
        name="cut_down",
    )(jnp.swapaxes(adapter_down, 1, 2))

    ends = jnp.cumsum(seg_tiles[0])
    positions = jnp.arange(tile_count, dtype=jnp.int32)
    segment = jnp.sum((positions[:, None] >= ends[None, :]).astype(jnp.int32), axis=1)
    seg_pick = segment[:, None] == jnp.arange(ends.shape[0], dtype=jnp.int32)[None, :]
    tile_adapter = jnp.sum(jnp.where(seg_pick, seg_adapter[:, 0][None, :], 0), axis=1)
    adapt_pick = tile_adapter[:, None] == jnp.arange(slots, dtype=jnp.int32)[None, :]
    tile_slot = jnp.sum(jnp.where(adapt_pick, owner_slot[None, :], 0), axis=1)
    core, owner = (tile_slot // n + my_data) % n_data, tile_slot % n
    tile_slot = core * n + owner
    tile_up = core * n + ((owner + my_inner) % inner) * outer + (my_outer - owner // inner) % outer

    def whole(*shape):
        return pl.BlockSpec(shape, lambda i, *_: (0,) * len(shape), pipeline_mode=once)

    def strip(wide, first=0):
        return pl.BlockSpec((block_rows, wide), lambda i, *_: (first + i, 0))

    def forward(c, sends):
        kept = outer if sends else n
        blocks, start = sizes[c], starts[c]
        chunk_rows = blocks * block_rows
        coded_spec = [pl.BlockSpec((outer, 1, held, cols), lambda i, *_: (0, i, 0, 0))]
        coded_shape = [jax.ShapeDtypeStruct((outer, blocks, held, cols), jnp.int16)]
        return pl.pallas_call(
            functools.partial(forward_kernel, start * (block_rows // TILE)),
            grid_spec=pltpu.PrefetchScalarGridSpec(
                num_scalar_prefetch=3,
                grid=(blocks,),
                in_specs=[
                    strip(width, start),
                    whole(width, out_width),
                    whole(n, rank, width),
                    whole(n, rank, width),
                    whole(n, rank, out_width),
                    whole(n, rank, out_width),
                ],
                out_specs=[
                    pl.BlockSpec((kept, block_rows, cols), lambda i, *_: (0, i, 0)),
                ]
                + coded_spec * sends,
                scratch_shapes=[
                    pltpu.VMEM((slots, 2 * rank, width), BF16),
                    pltpu.VMEM((slots, 2 * rank, out_width), BF16),
                ]
                + [pltpu.VMEM((n, block_rows, cols), F32)] * sends,
            ),
            out_shape=[
                jax.ShapeDtypeStruct((kept, chunk_rows, cols), F32),
            ]
            + coded_shape * sends,
            compiler_params=params,
            cost_estimate=pl.CostEstimate(
                flops=4 * chunk_rows * width * out_width, bytes_accessed=chunk_rows * width * 6, transcendentals=0
            ),
            name="forward",
        )(tile_slot, tile_up, place, tokens, frozen_weight, near_down, far_down, near_up, far_up)

    def swapped(x):
        return lax.ppermute(x, "mp", swap)

    def shifted(x):
        return lax.ppermute(x, "mp", ring)

    def behind(back):
        return lambda i, p: lax.rem(p[0] - back + outer, outer)

    def first(i, p):
        return 0

    def ring_step(s, kept, near, run):
        at = behind(s % outer)
        coded = [(near, at)] + [(r, first) for r in run]
        return add_parts(place, block_rows, 1, (kept, at), coded, last=s == outer)

    def pair_step(s, kept, run):
        at = behind(s)
        pick = (kept, lambda i, p: at(i, p) * inner + i)
        return add_parts(place, block_rows, inner, pick, [(r, lambda i, p: i) for r in run])

    def pair_end(kept, run, got):
        def whose(i, p):
            return p[1] if got else 1 - p[1]

        coded = [(run, whose)] + [(g, first) for g in got]
        return add_parts(place, block_rows, 1, (kept, lambda i, p: p[0] * inner + whose(i, p)), coded, last=bool(got))

    order = []
    for s in range(outer):
        at = ((my_outer - s) % outer) * inner
        order += [at + my_inner, at + other]
    cots = [cotangent, swapped(cotangent)]
    block, cots[-1], ups, cut = tie((shifted(cotangent), cots[-1], ups, cut))
    ups = jnp.concatenate(ups, axis=0)
    near_up = jnp.concatenate([ups, swapped(ups)], axis=0)
    near_down = lax.all_to_all(cut, "mp", split_axis=0, concat_axis=0, tiled=True)
    cots += [block, swapped(block)]
    if outer > 2:
        block = shifted(block)
    block, cots[-1], near_up, near_down = tie((block, cots[-1], near_up, near_down))
    far_up, far_down = (lax.ppermute(a, "dp", cores) for a in (near_up, near_down))
    own = rank // n
    half = rank // inner
    shrink = pl.pallas_call(
        shrink_kernel,
        grid_spec=pltpu.PrefetchScalarGridSpec(
            num_scalar_prefetch=1,
            grid=(steps // 2,),
            in_specs=[
                pl.BlockSpec((2 * block_rows, width), lambda i, s: (i, 0)),
                whole(n, rank, width),
                whole(n, rank, width),
            ],
            out_specs=pl.BlockSpec((rank, 2 * block_rows), lambda i, s: (0, i)),
            scratch_shapes=[pltpu.VMEM((slots, rank, width), BF16)],
        ),
        out_shape=jax.ShapeDtypeStruct((rank, rows), F32),
        compiler_params=params,
        cost_estimate=pl.CostEstimate(flops=0, bytes_accessed=rows * width * 2, transcendentals=0),
        name="shrink",
    )(tile_slot, tokens, near_down, far_down)
    mine = lax.dynamic_slice_in_dim(shrink, my_inner * half, half, 0)
    theirs = swapped(lax.dynamic_slice_in_dim(shrink, other * half, half, 0))
    parts = [forward(c, c < chunks - 1) for c in range(chunks)]
    near, outs = {}, {}
    runs = {c: [] for c in range(chunks)}

    done = {c: 0 for c in range(chunks)}

    def advance(c, through=outer):
        pair = c == chunks - 1
        while done[c] < min(through, outer - pair):
            done[c] += 1
            if pair:
                runs[c] = [shifted(pair_step(done[c], parts[c][0], runs[c]))]
                continue
            total = ring_step(done[c], parts[c][0], near[c], runs[c])
            if done[c] == outer:
                outs[c] = total
            else:
                runs[c] = [shifted(total)]

    last = chunks - 1
    for s in range(2, outer):
        cots += [block, swapped(block)]
        if s < outer - 1:
            block = shifted(block)
        if s == 2:
            block, cots[-1], parts[last], theirs = tie((block, cots[-1], parts[last], theirs))
    mine += theirs
    shrink = [lax.dynamic_slice_in_dim(mine, my_outer * own, own, 0)]
    for s in range(1, outer):
        theirs = lax.dynamic_slice_in_dim(mine, ((my_outer + s) % outer) * own, own, 0)
        shrink.append(lax.ppermute(theirs, "mp", [(i, (i + s * inner) % n) for i in range(n)]))
    advance(last, 1)
    cots[-1], parts[0], parts[1], runs, shrink = tie((cots[-1], parts[0], parts[1], runs, shrink))
    shrink = sum(shrink[1:], shrink[0])
    near[0] = swapped(parts[0][1])
    if cols % 128:
        natural = jnp.stack(cots)[jnp.argsort(jnp.stack(order))]
        cots = [jnp.transpose(natural, (1, 0, 2)).reshape(rows, out_width)]
    cot_all, back, gdown, rdown, gup, rup = pl.pallas_call(
        functools.partial(gradient_kernel, len(cots)),
        grid_spec=pltpu.PrefetchScalarGridSpec(
            num_scalar_prefetch=3,
            grid=(steps,),
            in_specs=[strip(a.shape[1]) for a in cots]
            + [strip(width), whole(n, rank, out_width), whole(n, rank, out_width)]
            + [pl.BlockSpec((own, block_rows), lambda i, *_: (0, i))],
            out_specs=[
                strip(out_width),
                strip(2 * rank),
                whole(n, rank, width),
                whole(n, rank, width),
                whole(n, own, out_width),
                whole(n, own, out_width),
            ],
            scratch_shapes=[
                pltpu.VMEM((slots, 2 * rank, out_width), BF16),
                pltpu.VMEM((block_rows, out_width), BF16),
                pltpu.VMEM((slots, rank, width), F32),
                pltpu.VMEM((slots, own, out_width), F32),
            ],
        ),
        out_shape=[
            jax.ShapeDtypeStruct((rows, out_width), BF16),
            jax.ShapeDtypeStruct((rows, 2 * rank), BF16),
            jax.ShapeDtypeStruct((n, rank, width), F32),
            jax.ShapeDtypeStruct((n, rank, width), F32),
            jax.ShapeDtypeStruct((n, own, out_width), F32),
            jax.ShapeDtypeStruct((n, own, out_width), F32),
        ],
        compiler_params=params,
        cost_estimate=pl.CostEstimate(
            flops=2 * rows * width * out_width, bytes_accessed=rows * (width * 2 + out_width * 4), transcendentals=0
        ),
        name="gradients",
    )(tile_slot, tile_up, jnp.stack(order).astype(jnp.int32), *cots, tokens, near_up, far_up, shrink)
    advance(last, 2)
    near[0], gdown, rdown, gup, rup, runs = tie((near[0], gdown, rdown, gup, rup, runs))
    near[1] = swapped(parts[1][1])
    advance(last)

    rdown = lax.ppermute(rdown, "dp", cores)
    rup = lax.ppermute(rup, "dp", cores)
    packed_rows = rank + PAD
    packed = pl.pallas_call(
        pack_kernel,
        grid=(n,),
        in_specs=[
            pl.BlockSpec((1, rank, width), lambda i: (i, 0, 0)),
            pl.BlockSpec((1, rank, width), lambda i: (i, 0, 0)),
            pl.BlockSpec((1, own, out_width), lambda i: (i, 0, 0)),
            pl.BlockSpec((1, own, out_width), lambda i: (i, 0, 0)),
        ],
        out_specs=pl.BlockSpec((1, packed_rows, width), lambda i: (i, 0, 0)),
        out_shape=jax.ShapeDtypeStruct((n, packed_rows, width), jnp.int16),
        name="pack_gradients",
    )(gdown, rdown, gup, rup)
    landed = lax.all_to_all(packed, "mp", split_axis=0, concat_axis=0, tiled=True)
    down_gradient, up_gradient = pl.pallas_call(
        unpack_kernel,
        grid=(n,),
        in_specs=[pl.BlockSpec((1, packed_rows, width), lambda i: (i, 0, 0))],
        out_specs=[
            pl.BlockSpec((1, rank, width), lambda i: (0, 0, i)),
            pl.BlockSpec((1, own, out_width), lambda i: ((i % inner) * outer + i // inner, 0, 0)),
        ],
        out_shape=[
            jax.ShapeDtypeStruct((1, rank, entire_width), F32),
            jax.ShapeDtypeStruct((n, own, out_width), F32),
        ],
        name="unpack_gradients",
    )(landed)

    token_gradient = pl.pallas_call(
        token_kernel,
        grid_spec=pltpu.PrefetchScalarGridSpec(
            num_scalar_prefetch=1,
            grid=(steps,),
            in_specs=[
                strip(out_width),
                whole(width, out_width),
                whole(n, rank, width),
                whole(n, rank, width),
                strip(2 * rank),
                pl.BlockSpec(memory_space=pl.ANY),
            ],
            out_specs=strip(width),
            scratch_shapes=[pltpu.VMEM((slots, 2 * rank, width), BF16)],
        ),
        out_shape=jax.ShapeDtypeStruct((rows, width), BF16),
        compiler_params=params,
        cost_estimate=pl.CostEstimate(
            flops=3 * rows * width * out_width, bytes_accessed=rows * (width * 2 + out_width * 2), transcendentals=0
        ),
        name="token_gradient",
    )(tile_slot, cot_all, frozen_weight, near_down, far_down, back, packed)
    kept, run = parts[last][0], runs[last][0]
    outs[last] = pair_end(kept, run, [swapped(pair_end(kept, run, []))])
    near, token_gradient = tie((near, token_gradient))
    for c in range(last):
        advance(c)
    output = jnp.concatenate([outs[c] for c in range(chunks)], axis=0)

    up_gradient = up_gradient.reshape(1, rank, out_width)
    return output, token_gradient, jnp.swapaxes(down_gradient, 1, 2), up_gradient


def solution(mesh):
    placed = (
        P(("groups", "dp"), "mp"),
        P("mp", None),
        P(("groups", "dp"), "mp"),
        P(("groups", "dp", "mp"), None, None),
        P(("groups", "dp", "mp"), None, None),
        P(("groups", "dp"), None),
        P(("groups", "dp"), None),
        P("groups"),
    )
    return jax.shard_map(
        body,
        mesh=mesh,
        in_specs=placed,
        out_specs=(
            P(("groups", "dp"), "mp"),
            P(("groups", "dp"), "mp"),
            P(("groups", "dp", "mp"), None, None),
            P(("groups", "dp", "mp"), None, None),
        ),
        check_vma=False,
    )
```

```python
import functools

import jax
import jax.numpy as jnp
from jax import lax
from jax.experimental import pallas as pl
from jax.experimental.pallas import tpu as pltpu
from jax.sharding import PartitionSpec as P

TILE = 128
ADAPTER_SCALE = 2.0
INNER = 2
PAD = 16
TOP = 32700.0
STEPS = 64.0
TINY = 1e-30
VMEM = 60 * 1024 * 1024
F32 = jnp.float32
BF16 = jnp.bfloat16
NT = (((1,), (1,)), ((), ()))
TN = (((0,), (0,)), ((), ()))


def dot(a, b, dims=(((1,), (0,)), ((), ()))):
    return lax.dot_general(a, b, dims, preferred_element_type=F32)


def split_halves(twice, rank):
    high = twice.astype(BF16).astype(F32)
    lane = lax.broadcasted_iota(jnp.int32, twice.shape, 1)
    return jnp.where(lane < rank, high, twice - high).astype(BF16)


def encode(v):
    most = jnp.max(jnp.abs(v), axis=0, keepdims=True)
    code = jnp.ceil(jnp.log2(jnp.maximum(most, TINY)) * STEPS)
    gain = jnp.exp2(code * (-1.0 / STEPS)) * TOP
    return jnp.round(v * gain).astype(jnp.int32).astype(jnp.int16), code


def step_of(code):
    return jnp.exp2(code.astype(jnp.int32).astype(F32) * (1.0 / STEPS)) * (1.0 / TOP)


def decode(q, code):
    return q.astype(jnp.int32).astype(F32) * step_of(code)


def copy_kernel(in_ref, out_ref):
    out_ref[...] = in_ref[...]


def fill_twice(pair_ref, near_ref, far_ref):
    n, rank = near_ref.shape[:2]
    for k, ref in enumerate((near_ref, far_ref)):
        pair_ref[k * n : (k + 1) * n, :rank, :] = ref[...]
        pair_ref[k * n : (k + 1) * n, rank:, :] = ref[...]


def forward_kernel(first, slot_ref, upslot_ref, place_ref, *refs):
    x_ref, w_ref, ndown_ref, fdown_ref, nup_ref, fup_ref, shrink_ref, kept_ref = refs[:8]
    *sent_refs, down_ref, up_ref, sum_ref = refs[8:] if len(refs) > 10 else (*refs[8:], kept_ref)
    step = pl.program_id(0)
    n, rows, cols = sum_ref.shape
    outer = kept_ref.shape[0]
    inner = n // outer
    tiles = rows // TILE
    rank = down_ref.shape[1] // 2

    @pl.when(step == 0)
    def _():
        fill_twice(down_ref, ndown_ref, fdown_ref)
        fill_twice(up_ref, nup_ref, fup_ref)

    base = dot(x_ref[...], w_ref[...])
    for t in range(tiles):
        at = slice(t * TILE, (t + 1) * TILE)
        tile = first + step * tiles + t
        shrink = dot(x_ref[at, :], down_ref[slot_ref[tile]], NT)
        shrink_ref[:, at] = shrink.T[:rank]
        pieces = split_halves(shrink, rank)
        total = base[at] + ADAPTER_SCALE * dot(pieces, up_ref[upslot_ref[tile]])
        for j in range(n):
            sum_ref[j, at, :] = total[:, j * cols : (j + 1) * cols]
    if not sent_refs:
        return
    mine = place_ref[1]
    for z in range(outer):
        kept_ref[z] = sum_ref[z * inner + mine]
    each = pl.num_programs(0) // len(sent_refs)
    for c, sent_ref in enumerate(sent_refs):

        @pl.when(step // each == c)
        def _(sent_ref=sent_ref):
            for z in range(outer):
                put(sent_ref.at[z, 0], *encode(sum_ref[z * inner + 1 - mine]))


def gradient_kernel(blocks, slot_ref, upslot_ref, order_ref, *refs):
    cots = refs[:blocks]
    x_ref, nup_ref, fup_ref, all_ref, back_ref, near_ref, far_ref, up_ref, cot_ref, sum_ref = refs[blocks:]
    step = pl.program_id(0)
    rows = x_ref.shape[0]
    tiles = rows // TILE
    rank = up_ref.shape[1] // 2

    @pl.when(step == 0)
    def _():
        fill_twice(up_ref, nup_ref, fup_ref)
        sum_ref[...] = jnp.zeros_like(sum_ref)

    for j, block in enumerate(cots):
        wide = block.shape[1]
        if blocks == 1:
            cot_ref[...] = block[...]
        else:
            cot_ref[:, pl.ds(pl.multiple_of(order_ref[j] * wide, wide), wide)] = block[...]
    all_ref[...] = cot_ref[...]
    for t in range(tiles):
        at = slice(t * TILE, (t + 1) * TILE)
        tile = step * tiles + t
        slot, cot = slot_ref[tile], cot_ref[at, :]
        pieces = split_halves(dot(cot, up_ref[upslot_ref[tile]], NT), rank)
        back_ref[at, :] = pieces
        grad = dot(pieces, x_ref[at, :], TN)
        sum_ref[slot] += grad[:rank] + grad[rank:]

    @pl.when(step == pl.num_programs(0) - 1)
    def _():
        n = near_ref.shape[0]
        near_ref[...] = sum_ref[:n]
        far_ref[...] = sum_ref[n:]


def up_kernel(slot_ref, shrink_ref, cot_ref, near_ref, far_ref, sum_ref):
    step = pl.program_id(0)
    own, rows = shrink_ref.shape
    tiles = rows // TILE

    @pl.when(step == 0)
    def _():
        sum_ref[...] = jnp.zeros_like(sum_ref)

    for t in range(tiles):
        at = slice(t * TILE, (t + 1) * TILE)
        slot, cot = slot_ref[step * tiles + t], cot_ref[at, :]
        shrink = shrink_ref[:, at]
        high = shrink.astype(BF16).astype(F32)
        low = shrink - high
        if own % 8:
            sum_ref[slot] += dot(high.astype(BF16), cot) + dot(low.astype(BF16), cot)
        else:
            grad = dot(jnp.concatenate([high, low], axis=0).astype(BF16), cot)
            sum_ref[slot] += grad[:own] + grad[own:]

    @pl.when(step == pl.num_programs(0) - 1)
    def _():
        n = near_ref.shape[0]
        near_ref[...] = sum_ref[:n]
        far_ref[...] = sum_ref[n:]


def token_kernel(slot_ref, cot_ref, w_ref, near_ref, far_ref, back_ref, out_ref, down_ref):
    step = pl.program_id(0)
    tiles = cot_ref.shape[0] // TILE

    @pl.when(step == 0)
    def _():
        fill_twice(down_ref, near_ref, far_ref)

    base = dot(cot_ref[...], w_ref[...], NT)
    for t in range(tiles):
        at = slice(t * TILE, (t + 1) * TILE)
        slot = slot_ref[step * tiles + t]
        out_ref[at, :] = (base[at] + ADAPTER_SCALE * dot(back_ref[at, :], down_ref[slot])).astype(BF16)


def put(ref, q, code):
    rows = q.shape[0]
    ref[:rows, :] = q
    ref[rows:, :] = jnp.broadcast_to(code, (PAD, code.shape[1])).astype(jnp.int32).astype(jnp.int16)


def sum_kernel(coded, place_ref, *refs):
    total = refs[0][0]
    rows = total.shape[0]
    for ref in refs[1 : 1 + coded]:
        total = total + decode(ref[0, 0, :rows, :], ref[0, 0, rows : rows + 1, :])
    out_ref = refs[-1]
    if out_ref.dtype == BF16:
        out_ref[...] = total.astype(BF16)
    else:
        put(out_ref.at[0, 0], *encode(total))


def add_parts(place, block_rows, count, kept, coded, first=0, blocks=None, last=False):
    part, pick = kept
    rows, cols = part.shape[1:]
    blocks, held = blocks or rows // block_rows, block_rows + PAD
    rows = blocks * block_rows

    def coded_spec(pick):
        return pl.BlockSpec((1, 1, held, cols), lambda i, b, p: (pick(i, p), b, 0, 0))

    in_specs = [pl.BlockSpec((1, block_rows, cols), lambda i, b, p: (pick(i, p), first + b, 0))]
    in_specs += [coded_spec(q) for _, q in coded]
    if last:
        out_shape = jax.ShapeDtypeStruct((rows, cols), BF16)
        out_spec = pl.BlockSpec((block_rows, cols), lambda i, b, p: (b, 0))
    else:
        out_shape = jax.ShapeDtypeStruct((count, blocks, held, cols), jnp.int16)
        out_spec = coded_spec(lambda i, p: i)
    return pl.pallas_call(
        functools.partial(sum_kernel, len(coded)),
        grid_spec=pltpu.PrefetchScalarGridSpec(
            num_scalar_prefetch=1, grid=(count, blocks), in_specs=in_specs, out_specs=out_spec
        ),
        out_shape=out_shape,
        cost_estimate=pl.CostEstimate(flops=0, bytes_accessed=count * rows * cols * 8, transcendentals=0),
        name="add_parts",
    )(place, part, *[a for a, _ in coded])


def pack_kernel(gdown_ref, rdown_ref, gup_ref, rup_ref, out_ref):
    rank, width = gdown_ref.shape[1:]
    own = gup_ref.shape[1]
    groups = gup_ref.shape[2] // width
    q, code = encode(gdown_ref[0] + rdown_ref[0])
    out_ref[0, :rank, :] = q
    tail, codes = [], [code]
    up = gup_ref[0] + rup_ref[0]
    for g in range(groups):
        q, code = encode(up[:, g * width : (g + 1) * width])
        tail.append(q.astype(jnp.int32))
        codes.append(code)
    row = lax.broadcasted_iota(jnp.int32, (PAD - groups * own, width), 0)
    last = jnp.zeros(row.shape, F32)
    for g, code in enumerate(codes):
        last = jnp.where(row == g, code, last)
    out_ref[0, rank:, :] = jnp.concatenate([*tail, last.astype(jnp.int32)], axis=0).astype(jnp.int16)


def unpack_kernel(in_ref, down_ref, up_ref):
    width = in_ref.shape[2]
    own = up_ref.shape[1]
    groups = up_ref.shape[2] // width
    rank = down_ref.shape[1]
    tail = in_ref[0, rank:, :].astype(jnp.int32).astype(F32)
    steps = jnp.exp2(tail[groups * own :] * (1.0 / STEPS)) * (ADAPTER_SCALE / TOP)
    down_ref[0] = in_ref[0, :rank, :].astype(jnp.int32).astype(F32) * steps[:1]
    for g in range(groups):
        up_ref[0, :, g * width : (g + 1) * width] = tail[g * own : (g + 1) * own] * steps[g + 1 : g + 2]


def body(
    tokens, frozen_weight, cotangent, adapter_down, adapter_up, seg_tiles, seg_adapter, owner_slot
):
    rows, width = tokens.shape
    cols = cotangent.shape[1]
    n = lax.axis_size("mp")
    n_data = lax.axis_size("dp")
    _, entire_width, rank = adapter_down.shape
    out_width = adapter_up.shape[2]
    slots = n_data * n
    tile_count = rows // TILE
    inner = INNER
    outer = n // inner
    me = lax.axis_index("mp")
    my_outer, my_inner = me // inner, me % inner
    other = 1 - my_inner
    my_data = lax.axis_index("dp")
    swap = [(i, i ^ 1) for i in range(n)]
    ring = [(i, (i + inner) % n) for i in range(n)]
    cores = [(i, 1 - i) for i in range(n_data)]

    place = jnp.stack([my_outer, my_inner]).astype(jnp.int32)

    block_rows = 8 * TILE
    steps = rows // block_rows
    each = steps // 4
    last = 2
    once = pl.Buffered(1)
    params = pltpu.CompilerParams(vmem_limit_bytes=VMEM)
    held = block_rows + PAD
    tie = lax.optimization_barrier

    ups = [adapter_up]
    for s in range(1, outer):
        ups.append(lax.ppermute(adapter_up, "mp", [(i, (i + s * inner) % n) for i in range(n)]))
    cut = pl.pallas_call(
        copy_kernel,
        grid=(n,),
        in_specs=[pl.BlockSpec((1, rank, width), lambda i: (0, 0, i))],
        out_specs=pl.BlockSpec((1, rank, width), lambda i: (i, 0, 0)),
        out_shape=jax.ShapeDtypeStruct((n, rank, width), BF16),
        name="cut_down",
    )(jnp.swapaxes(adapter_down, 1, 2))

    ends = jnp.cumsum(seg_tiles[0])
    positions = jnp.arange(tile_count, dtype=jnp.int32)
    segment = jnp.sum((positions[:, None] >= ends[None, :]).astype(jnp.int32), axis=1)
    seg_pick = segment[:, None] == jnp.arange(ends.shape[0], dtype=jnp.int32)[None, :]
    tile_adapter = jnp.sum(jnp.where(seg_pick, seg_adapter[:, 0][None, :], 0), axis=1)
    adapt_pick = tile_adapter[:, None] == jnp.arange(slots, dtype=jnp.int32)[None, :]
    tile_slot = jnp.sum(jnp.where(adapt_pick, owner_slot[None, :], 0), axis=1)
    core, owner = (tile_slot // n + my_data) % n_data, tile_slot % n
    tile_slot = core * n + owner
    tile_up = core * n + ((owner + my_inner) % inner) * outer + (my_outer - owner // inner) % outer

    def whole(*shape):
        return pl.BlockSpec(shape, lambda i, *_: (0,) * len(shape), pipeline_mode=once)

    def strip(wide, first=0):
        return pl.BlockSpec((block_rows, wide), lambda i, *_: (first + i, 0))

    def forward(start, count, chunks):
        kept = outer if chunks else n
        each = count // max(chunks, 1)
        coded_specs = [
            pl.BlockSpec((outer, 1, held, cols), lambda i, *_, c=c: (0, jnp.clip(i - c * each, 0, each - 1), 0, 0))
            for c in range(chunks)
        ]
        return pl.pallas_call(
            functools.partial(forward_kernel, start * (block_rows // TILE)),
            grid_spec=pltpu.PrefetchScalarGridSpec(
                num_scalar_prefetch=3,
                grid=(count,),
                in_specs=[
                    strip(width, start),
                    whole(width, out_width),
                    whole(n, rank, width),
                    whole(n, rank, width),
                    whole(n, rank, out_width),
                    whole(n, rank, out_width),
                ],
                out_specs=[
                    pl.BlockSpec((rank, block_rows), lambda i, *_: (0, i)),
                    pl.BlockSpec((kept, block_rows, cols), lambda i, *_: (0, i, 0)),
                    *coded_specs,
                ],
                scratch_shapes=[
                    pltpu.VMEM((slots, 2 * rank, width), BF16),
                    pltpu.VMEM((slots, 2 * rank, out_width), BF16),
                ]
                + [pltpu.VMEM((n, block_rows, cols), F32)] * (chunks > 0),
            ),
            out_shape=[
                jax.ShapeDtypeStruct((rank, count * block_rows), F32),
                jax.ShapeDtypeStruct((kept, count * block_rows, cols), F32),
                *[jax.ShapeDtypeStruct((outer, each, held, cols), jnp.int16)] * chunks,
            ],
            compiler_params=params,
            cost_estimate=pl.CostEstimate(
                flops=4 * count * block_rows * width * out_width,
                bytes_accessed=count * block_rows * width * 6,
                transcendentals=0,
            ),
            name="forward",
        )(tile_slot, tile_up, place, tokens, frozen_weight, near_down, far_down, near_up, far_up)

    def swapped(x):
        return lax.ppermute(x, "mp", swap)

    def shifted(x):
        return lax.ppermute(x, "mp", ring)

    def behind(back):
        return lambda i, p: lax.rem(p[0] - back + outer, outer)

    def first(i, p):
        return 0

    def ring_step(s, kept, near, run, c):
        at = behind(s % outer)
        coded = [(near, at)] + [(r, first) for r in run]
        return add_parts(place, block_rows, 1, (kept, at), coded, c * each, each, last=s == outer)

    def pair_step(s, kept, run):
        at = behind(s)
        pick = (kept, lambda i, p: at(i, p) * inner + i)
        return add_parts(place, block_rows, inner, pick, [(r, lambda i, p: i) for r in run])

    def pair_end(kept, run, got):
        def whose(i, p):
            return p[1] if got else 1 - p[1]

        coded = [(run, whose)] + [(g, first) for g in got]
        return add_parts(place, block_rows, 1, (kept, lambda i, p: p[0] * inner + whose(i, p)), coded, last=bool(got))

    order = []
    for s in range(outer):
        at = ((my_outer - s) % outer) * inner
        order += [at + my_inner, at + other]
    cots = [cotangent, swapped(cotangent)]
    block, cots[-1], ups, cut = tie((shifted(cotangent), cots[-1], ups, cut))
    ups = jnp.concatenate(ups, axis=0)
    near_up = jnp.concatenate([ups, swapped(ups)], axis=0)
    near_down = lax.all_to_all(cut, "mp", split_axis=0, concat_axis=0, tiled=True)
    cots += [block, swapped(block)]
    if outer > 2:
        block = shifted(block)
    block, cots[-1], near_up, near_down = tie((block, cots[-1], near_up, near_down))
    far_up, far_down = (lax.ppermute(a, "dp", cores) for a in (near_up, near_down))
    own = rank // n
    half = rank // inner
    late_shrink, pair = forward(2 * each, steps - 2 * each, 0)
    shrink, kept, *sents = forward(0, 2 * each, 2)
    near, outs, runs, sums, done = {}, {}, [()] * 3, [()] * 3, [0] * 3

    def add(*chunks):
        for c in chunks:
            done[c] += 1
            if c == last:
                sums[c] = pair_step(done[c], pair, runs[c])
            else:
                sums[c] = ring_step(done[c], kept, near[c], runs[c], c)

    def send(*chunks):
        for c in chunks:
            runs[c] = (shifted(sums[c]),)

    for s in range(2, outer):
        cots += [block, swapped(block)]
        if s < outer - 1:
            block = shifted(block)
        if s == 2:
            add(last)
            block, cots[-1], sums[last] = tie((block, cots[-1], sums[last]))
    send(last)
    cots[-1], kept, sents, runs, shrink = tie((cots[-1], kept, sents, runs, shrink))

    shrink = jnp.concatenate([shrink, late_shrink], axis=1)
    theirs = swapped(lax.dynamic_slice_in_dim(shrink, other * half, half, 0))
    add(last)
    mine = lax.dynamic_slice_in_dim(shrink, my_inner * half, half, 0) + theirs
    send(last)
    cots[-1], mine = tie((cots[-1], mine))
    shrink = [lax.dynamic_slice_in_dim(mine, my_outer * own, own, 0)]
    for s in range(1, outer):
        theirs = lax.dynamic_slice_in_dim(mine, ((my_outer + s) % outer) * own, own, 0)
        shrink.append(lax.ppermute(theirs, "mp", [(i, (i + s * inner) % n) for i in range(n)]))
    near[0] = swapped(sents[0])

    if cols % 128:
        natural = jnp.stack(cots)[jnp.argsort(jnp.stack(order))]
        cots = [jnp.transpose(natural, (1, 0, 2)).reshape(rows, out_width)]
    cot_all, back, gdown, rdown = pl.pallas_call(
        functools.partial(gradient_kernel, len(cots)),
        grid_spec=pltpu.PrefetchScalarGridSpec(
            num_scalar_prefetch=3,
            grid=(steps,),
            in_specs=[strip(a.shape[1]) for a in cots]
            + [strip(width), whole(n, rank, out_width), whole(n, rank, out_width)],
            out_specs=[
                strip(out_width),
                strip(2 * rank),
                whole(n, rank, width),
                whole(n, rank, width),
            ],
            scratch_shapes=[
                pltpu.VMEM((slots, 2 * rank, out_width), BF16),
                pltpu.VMEM((block_rows, out_width), BF16),
                pltpu.VMEM((slots, rank, width), F32),
            ],
        ),
        out_shape=[
            jax.ShapeDtypeStruct((rows, out_width), BF16),
            jax.ShapeDtypeStruct((rows, 2 * rank), BF16),
            jax.ShapeDtypeStruct((n, rank, width), F32),
            jax.ShapeDtypeStruct((n, rank, width), F32),
        ],
        compiler_params=params,
        cost_estimate=pl.CostEstimate(
            flops=2 * rows * width * out_width, bytes_accessed=rows * (width * 2 + out_width * 4), transcendentals=0
        ),
        name="gradients",
    )(tile_slot, tile_up, jnp.stack(order).astype(jnp.int32), *cots, tokens, near_up, far_up)
    near[0], gdown, rdown, runs, shrink = tie((near[0], gdown, rdown, runs, shrink))
    shrink = sum(shrink[1:], shrink[0])
    near[1] = swapped(sents[1])
    add(0)
    sums, near[0] = tie((sums, near[0]))
    send(0)
    while done[last] < outer - 1:
        add(last)
        send(last)

    gup, rup = pl.pallas_call(
        up_kernel,
        grid_spec=pltpu.PrefetchScalarGridSpec(
            num_scalar_prefetch=1,
            grid=(steps,),
            in_specs=[pl.BlockSpec((own, block_rows), lambda i, s: (0, i)), strip(out_width)],
            out_specs=[whole(n, own, out_width), whole(n, own, out_width)],
            scratch_shapes=[pltpu.VMEM((slots, own, out_width), F32)],
        ),
        out_shape=[
            jax.ShapeDtypeStruct((n, own, out_width), F32),
            jax.ShapeDtypeStruct((n, own, out_width), F32),
        ],
        compiler_params=params,
        cost_estimate=pl.CostEstimate(flops=0, bytes_accessed=rows * out_width * 2, transcendentals=0),
        name="up_gradient",
    )(tile_slot, shrink, cot_all)
    rdown = lax.ppermute(rdown, "dp", cores)
    rup = lax.ppermute(rup, "dp", cores)
    packed_rows = rank + PAD
    packed = pl.pallas_call(
        pack_kernel,
        grid=(n,),
        in_specs=[
            pl.BlockSpec((1, rank, width), lambda i: (i, 0, 0)),
            pl.BlockSpec((1, rank, width), lambda i: (i, 0, 0)),
            pl.BlockSpec((1, own, out_width), lambda i: (i, 0, 0)),
            pl.BlockSpec((1, own, out_width), lambda i: (i, 0, 0)),
        ],
        out_specs=pl.BlockSpec((1, packed_rows, width), lambda i: (i, 0, 0)),
        out_shape=jax.ShapeDtypeStruct((n, packed_rows, width), jnp.int16),
        name="pack_gradients",
    )(gdown, rdown, gup, rup)
    near, packed = tie((near, packed))
    add(1)
    send(1)
    runs, packed = tie((runs, packed))
    landed = lax.all_to_all(packed, "mp", split_axis=0, concat_axis=0, tiled=True)
    down_gradient, up_gradient = pl.pallas_call(
        unpack_kernel,
        grid=(n,),
        in_specs=[pl.BlockSpec((1, packed_rows, width), lambda i: (i, 0, 0))],
        out_specs=[
            pl.BlockSpec((1, rank, width), lambda i: (0, 0, i)),
            pl.BlockSpec((1, own, out_width), lambda i: ((i % inner) * outer + i // inner, 0, 0)),
        ],
        out_shape=[
            jax.ShapeDtypeStruct((1, rank, entire_width), F32),
            jax.ShapeDtypeStruct((n, own, out_width), F32),
        ],
        name="unpack_gradients",
    )(landed)

    token_gradient = pl.pallas_call(
        token_kernel,
        grid_spec=pltpu.PrefetchScalarGridSpec(
            num_scalar_prefetch=1,
            grid=(steps,),
            in_specs=[
                strip(out_width),
                whole(width, out_width),
                whole(n, rank, width),
                whole(n, rank, width),
                strip(2 * rank),
            ],
            out_specs=strip(width),
            scratch_shapes=[pltpu.VMEM((slots, 2 * rank, width), BF16)],
        ),
        out_shape=jax.ShapeDtypeStruct((rows, width), BF16),
        compiler_params=params,
        cost_estimate=pl.CostEstimate(
            flops=3 * rows * width * out_width, bytes_accessed=rows * (width * 2 + out_width * 2), transcendentals=0
        ),
        name="token_gradient",
    )(tile_slot, cot_all, frozen_weight, near_down, far_down, back)
    run = runs[last][0]
    outs[last] = pair_end(pair, run, [swapped(pair_end(pair, run, []))])
    add(0)
    send(0)
    runs, outs, token_gradient = tie((runs, outs, token_gradient))
    for c in (1, 0):
        add(c)
        send(c)
    runs, down_gradient, up_gradient = tie((runs, down_gradient, up_gradient))
    while done[1] < outer:
        for c in (1, 0):
            if done[c] < outer:
                add(c)
                if done[c] < outer:
                    send(c)
    output = jnp.concatenate([sums[0], sums[1], outs[last]], axis=0)

    up_gradient = up_gradient.reshape(1, rank, out_width)
    return output, token_gradient, jnp.swapaxes(down_gradient, 1, 2), up_gradient


def solution(mesh):
    placed = (
        P(("groups", "dp"), "mp"),
        P("mp", None),
        P(("groups", "dp"), "mp"),
        P(("groups", "dp", "mp"), None, None),
        P(("groups", "dp", "mp"), None, None),
        P(("groups", "dp"), None),
        P(("groups", "dp"), None),
        P("groups"),
    )
    return jax.shard_map(
        body,
        mesh=mesh,
        in_specs=placed,
        out_specs=(
            P(("groups", "dp"), "mp"),
            P(("groups", "dp"), "mp"),
            P(("groups", "dp", "mp"), None, None),
            P(("groups", "dp", "mp"), None, None),
        ),
        check_vma=False,
    )
```

```python
import functools

import jax
import jax.numpy as jnp
from jax import lax
from jax.experimental import pallas as pl
from jax.experimental.pallas import tpu as pltpu
from jax.sharding import PartitionSpec as P

TILE = 128
ADAPTER_SCALE = 2.0
INNER = 2
PAD = 16
TOP = 32700.0
STEPS = 64.0
TINY = 1e-30
VMEM = 60 * 1024 * 1024
F32 = jnp.float32
BF16 = jnp.bfloat16
NT = (((1,), (1,)), ((), ()))
TN = (((0,), (0,)), ((), ()))


def dot(a, b, dims=(((1,), (0,)), ((), ()))):
    return lax.dot_general(a, b, dims, preferred_element_type=F32)


def split_halves(twice, rank):
    high = twice.astype(BF16).astype(F32)
    lane = lax.broadcasted_iota(jnp.int32, twice.shape, 1)
    return jnp.where(lane < rank, high, twice - high).astype(BF16)


def encode(v):
    most = jnp.max(jnp.abs(v), axis=0, keepdims=True)
    code = jnp.ceil(jnp.log2(jnp.maximum(most, TINY)) * STEPS)
    gain = jnp.exp2(code * (-1.0 / STEPS)) * TOP
    return jnp.round(v * gain).astype(jnp.int32).astype(jnp.int16), code


def step_of(code):
    return jnp.exp2(code.astype(jnp.int32).astype(F32) * (1.0 / STEPS)) * (1.0 / TOP)


def decode(q, code):
    return q.astype(jnp.int32).astype(F32) * step_of(code)


def copy_kernel(in_ref, out_ref):
    out_ref[...] = in_ref[...]


def fill_twice(pair_ref, near_ref, far_ref):
    n, rank = near_ref.shape[:2]
    for k, ref in enumerate((near_ref, far_ref)):
        pair_ref[k * n : (k + 1) * n, :rank, :] = ref[...]
        pair_ref[k * n : (k + 1) * n, rank:, :] = ref[...]


def forward_kernel(first, slot_ref, upslot_ref, place_ref, *refs):
    x_ref, w_ref, ndown_ref, fdown_ref, nup_ref, fup_ref, shrink_ref, kept_ref = refs[:8]
    *sent_refs, down_ref, up_ref, sum_ref = refs[8:] if len(refs) > 10 else (*refs[8:], kept_ref)
    step = pl.program_id(0)
    n, rows, cols = sum_ref.shape
    outer = kept_ref.shape[0]
    inner = n // outer
    tiles = rows // TILE
    rank = down_ref.shape[1] // 2

    @pl.when(step == 0)
    def _():
        fill_twice(down_ref, ndown_ref, fdown_ref)
        fill_twice(up_ref, nup_ref, fup_ref)

    base = dot(x_ref[...], w_ref[...])
    for t in range(tiles):
        at = slice(t * TILE, (t + 1) * TILE)
        tile = first + step * tiles + t
        shrink = dot(x_ref[at, :], down_ref[slot_ref[tile]], NT)
        shrink_ref[:, at] = shrink.T[:rank]
        pieces = split_halves(shrink, rank)
        total = base[at] + ADAPTER_SCALE * dot(pieces, up_ref[upslot_ref[tile]])
        for j in range(n):
            sum_ref[j, at, :] = total[:, j * cols : (j + 1) * cols]
    if not sent_refs:
        return
    mine = place_ref[1]
    for z in range(outer):
        kept_ref[z] = sum_ref[z * inner + mine]
    each = pl.num_programs(0) // len(sent_refs)
    for c, sent_ref in enumerate(sent_refs):

        @pl.when(step // each == c)
        def _(sent_ref=sent_ref):
            for z in range(outer):
                put(sent_ref.at[z, 0], *encode(sum_ref[z * inner + 1 - mine]))


def gradient_kernel(blocks, slot_ref, upslot_ref, order_ref, *refs):
    cots = refs[:blocks]
    x_ref, nup_ref, fup_ref, all_ref, back_ref, near_ref, far_ref, up_ref, cot_ref, sum_ref = refs[blocks:]
    step = pl.program_id(0)
    rows = x_ref.shape[0]
    tiles = rows // TILE
    rank = up_ref.shape[1] // 2

    @pl.when(step == 0)
    def _():
        fill_twice(up_ref, nup_ref, fup_ref)
        sum_ref[...] = jnp.zeros_like(sum_ref)

    for j, block in enumerate(cots):
        wide = block.shape[1]
        if blocks == 1:
            cot_ref[...] = block[...]
        else:
            cot_ref[:, pl.ds(pl.multiple_of(order_ref[j] * wide, wide), wide)] = block[...]
    all_ref[...] = cot_ref[...]
    for t in range(tiles):
        at = slice(t * TILE, (t + 1) * TILE)
        tile = step * tiles + t
        slot, cot = slot_ref[tile], cot_ref[at, :]
        pieces = split_halves(dot(cot, up_ref[upslot_ref[tile]], NT), rank)
        back_ref[at, :] = pieces
        grad = dot(pieces, x_ref[at, :], TN)
        sum_ref[slot] += grad[:rank] + grad[rank:]

    @pl.when(step == pl.num_programs(0) - 1)
    def _():
        n = near_ref.shape[0]
        near_ref[...] = sum_ref[:n]
        far_ref[...] = sum_ref[n:]


def up_kernel(slot_ref, shrink_ref, cot_ref, near_ref, far_ref, sum_ref):
    step = pl.program_id(0)
    own, rows = shrink_ref.shape
    tiles = rows // TILE

    @pl.when(step == 0)
    def _():
        sum_ref[...] = jnp.zeros_like(sum_ref)

    for t in range(tiles):
        at = slice(t * TILE, (t + 1) * TILE)
        slot, cot = slot_ref[step * tiles + t], cot_ref[at, :]
        shrink = shrink_ref[:, at]
        high = shrink.astype(BF16).astype(F32)
        low = shrink - high
        if own % 8:
            sum_ref[slot] += dot(high.astype(BF16), cot) + dot(low.astype(BF16), cot)
        else:
            grad = dot(jnp.concatenate([high, low], axis=0).astype(BF16), cot)
            sum_ref[slot] += grad[:own] + grad[own:]

    @pl.when(step == pl.num_programs(0) - 1)
    def _():
        n = near_ref.shape[0]
        near_ref[...] = sum_ref[:n]
        far_ref[...] = sum_ref[n:]


def token_kernel(slot_ref, cot_ref, w_ref, near_ref, far_ref, back_ref, out_ref, down_ref):
    step = pl.program_id(0)
    tiles = cot_ref.shape[0] // TILE

    @pl.when(step == 0)
    def _():
        fill_twice(down_ref, near_ref, far_ref)

    base = dot(cot_ref[...], w_ref[...], NT)
    for t in range(tiles):
        at = slice(t * TILE, (t + 1) * TILE)
        slot = slot_ref[step * tiles + t]
        out_ref[at, :] = (base[at] + ADAPTER_SCALE * dot(back_ref[at, :], down_ref[slot])).astype(BF16)


def put(ref, q, code):
    rows = q.shape[0]
    ref[:rows, :] = q
    ref[rows:, :] = jnp.broadcast_to(code, (PAD, code.shape[1])).astype(jnp.int32).astype(jnp.int16)


def sum_kernel(coded, each, place_ref, *refs):
    total = refs[0][0]
    rows = total.shape[0]
    refs = list(refs[1:])
    for count in coded:
        values = [decode(ref[0, 0, :rows, :], ref[0, 0, rows : rows + 1, :]) for ref in refs[:count]]
        total = total + (jnp.where(pl.program_id(1) < each, *values) if count == 2 else values[0])
        refs = refs[count:]
    out_ref = refs[-1]
    if out_ref.dtype == BF16:
        out_ref[...] = total.astype(BF16)
    else:
        put(out_ref.at[0, 0], *encode(total))


def add_parts(place, block_rows, count, kept, coded, first=0, blocks=None, last=None, beside=()):
    part, pick = kept
    rows, cols = part.shape[1:]
    blocks, held = blocks or rows // block_rows, block_rows + PAD
    rows = blocks * block_rows

    def coded_spec(pick, start=0, size=blocks):
        return pl.BlockSpec(
            (1, 1, held, cols), lambda i, b, p: (pick(i, p), jnp.clip(b - start, 0, size - 1) if size < blocks else b, 0, 0)
        )

    in_specs = [pl.BlockSpec((1, block_rows, cols), lambda i, b, p: (pick(i, p), first + b, 0))]
    arrays, counts = [], []
    for held_in, q in coded:
        held_in = held_in if isinstance(held_in, tuple) else (held_in,)
        size = blocks // len(held_in)
        in_specs += [coded_spec(q, k * size, size) for k in range(len(held_in))]
        arrays += held_in
        counts.append(len(held_in))
    if last is not None:
        out_shape = jax.ShapeDtypeStruct((2 * rows, cols), BF16)
        out_spec = pl.BlockSpec((block_rows, cols), lambda i, b, p: (last + b, 0))
    else:
        out_shape = jax.ShapeDtypeStruct((count, blocks, held, cols), jnp.int16)
        out_spec = coded_spec(lambda i, p: i)
    return pl.pallas_call(
        functools.partial(sum_kernel, tuple(counts), blocks // 2),
        grid_spec=pltpu.PrefetchScalarGridSpec(
            num_scalar_prefetch=1,
            grid=(count, blocks),
            in_specs=in_specs + [pl.BlockSpec(memory_space=pl.ANY)] * len(beside),
            out_specs=out_spec,
        ),
        out_shape=out_shape,
        input_output_aliases={2 + len(arrays): 0} if beside else {},
        cost_estimate=pl.CostEstimate(flops=0, bytes_accessed=count * rows * cols * 8, transcendentals=0),
        name="add_parts",
    )(place, part, *arrays, *beside)


def pack_kernel(gdown_ref, rdown_ref, gup_ref, rup_ref, out_ref):
    count, rank, width = gdown_ref.shape
    own = gup_ref.shape[1]
    groups = gup_ref.shape[2] // width
    row = lax.broadcasted_iota(jnp.int32, (PAD - groups * own, width), 0)
    for s in range(count):
        q, code = encode(gdown_ref[s] + rdown_ref[s])
        out_ref[s, :rank, :] = q
        tail, codes = [], [code]
        up = gup_ref[s] + rup_ref[s]
        for g in range(groups):
            q, code = encode(up[:, g * width : (g + 1) * width])
            tail.append(q.astype(jnp.int32))
            codes.append(code)
        last = jnp.zeros(row.shape, F32)
        for g, code in enumerate(codes):
            last = jnp.where(row == g, code, last)
        out_ref[s, rank:, :] = jnp.concatenate([*tail, last.astype(jnp.int32)], axis=0).astype(jnp.int16)


def unpack_kernel(outer, in_ref, down_ref, up_ref):
    count, _, width = in_ref.shape
    n, own, out_width = up_ref.shape
    groups = out_width // width
    rank = down_ref.shape[1]
    for s in range(count):
        source = pl.program_id(0) * count + s
        tail = in_ref[s, rank:, :].astype(jnp.int32).astype(F32)
        steps = jnp.exp2(tail[groups * own :] * (1.0 / STEPS)) * (ADAPTER_SCALE / TOP)
        down_ref[0, :, s * width : (s + 1) * width] = in_ref[s, :rank, :].astype(jnp.int32).astype(F32) * steps[:1]
        place = (source % (n // outer)) * outer + source // (n // outer)
        for g in range(groups):
            up_ref[place, :, g * width : (g + 1) * width] = tail[g * own : (g + 1) * own] * steps[g + 1 : g + 2]


def body(
    tokens, frozen_weight, cotangent, adapter_down, adapter_up, seg_tiles, seg_adapter, owner_slot
):
    rows, width = tokens.shape
    cols = cotangent.shape[1]
    n = lax.axis_size("mp")
    n_data = lax.axis_size("dp")
    _, entire_width, rank = adapter_down.shape
    out_width = adapter_up.shape[2]
    slots = n_data * n
    tile_count = rows // TILE
    inner = INNER
    outer = n // inner
    me = lax.axis_index("mp")
    my_outer, my_inner = me // inner, me % inner
    other = 1 - my_inner
    my_data = lax.axis_index("dp")
    swap = [(i, i ^ 1) for i in range(n)]
    ring = [(i, (i + inner) % n) for i in range(n)]
    cores = [(i, 1 - i) for i in range(n_data)]

    place = jnp.stack([my_outer, my_inner]).astype(jnp.int32)

    block_rows = 8 * TILE
    steps = rows // block_rows
    each = steps // 4
    last = 2
    once = pl.Buffered(1)
    params = pltpu.CompilerParams(vmem_limit_bytes=VMEM)
    held = block_rows + PAD
    tie = lax.optimization_barrier

    ups = [adapter_up]
    for s in range(1, outer):
        ups.append(lax.ppermute(adapter_up, "mp", [(i, (i + s * inner) % n) for i in range(n)]))
    cut = pl.pallas_call(
        copy_kernel,
        grid=(n,),
        in_specs=[pl.BlockSpec((1, rank, width), lambda i: (0, 0, i))],
        out_specs=pl.BlockSpec((1, rank, width), lambda i: (i, 0, 0)),
        out_shape=jax.ShapeDtypeStruct((n, rank, width), BF16),
        name="cut_down",
    )(jnp.swapaxes(adapter_down, 1, 2))

    ends = jnp.cumsum(seg_tiles[0])
    positions = jnp.arange(tile_count, dtype=jnp.int32)
    segment = jnp.sum((positions[:, None] >= ends[None, :]).astype(jnp.int32), axis=1)
    seg_pick = segment[:, None] == jnp.arange(ends.shape[0], dtype=jnp.int32)[None, :]
    tile_adapter = jnp.sum(jnp.where(seg_pick, seg_adapter[:, 0][None, :], 0), axis=1)
    adapt_pick = tile_adapter[:, None] == jnp.arange(slots, dtype=jnp.int32)[None, :]
    tile_slot = jnp.sum(jnp.where(adapt_pick, owner_slot[None, :], 0), axis=1)
    core, owner = (tile_slot // n + my_data) % n_data, tile_slot % n
    tile_slot = core * n + owner
    tile_up = core * n + ((owner + my_inner) % inner) * outer + (my_outer - owner // inner) % outer

    def whole(*shape):
        return pl.BlockSpec(shape, lambda i, *_: (0,) * len(shape), pipeline_mode=once)

    def strip(wide, first=0):
        return pl.BlockSpec((block_rows, wide), lambda i, *_: (first + i, 0))

    def forward(start, count, chunks):
        kept = outer if chunks else n
        each = count // max(chunks, 1)
        coded_specs = [
            pl.BlockSpec((outer, 1, held, cols), lambda i, *_, c=c: (0, jnp.clip(i - c * each, 0, each - 1), 0, 0))
            for c in range(chunks)
        ]
        return pl.pallas_call(
            functools.partial(forward_kernel, start * (block_rows // TILE)),
            grid_spec=pltpu.PrefetchScalarGridSpec(
                num_scalar_prefetch=3,
                grid=(count,),
                in_specs=[
                    strip(width, start),
                    whole(width, out_width),
                    whole(n, rank, width),
                    whole(n, rank, width),
                    whole(n, rank, out_width),
                    whole(n, rank, out_width),
                ],
                out_specs=[
                    pl.BlockSpec((rank, block_rows), lambda i, *_: (0, i)),
                    pl.BlockSpec((kept, block_rows, cols), lambda i, *_: (0, i, 0)),
                    *coded_specs,
                ],
                scratch_shapes=[
                    pltpu.VMEM((slots, 2 * rank, width), BF16),
                    pltpu.VMEM((slots, 2 * rank, out_width), BF16),
                ]
                + [pltpu.VMEM((n, block_rows, cols), F32)] * (chunks > 0),
            ),
            out_shape=[
                jax.ShapeDtypeStruct((rank, count * block_rows), F32),
                jax.ShapeDtypeStruct((kept, count * block_rows, cols), F32),
                *[jax.ShapeDtypeStruct((outer, each, held, cols), jnp.int16)] * chunks,
            ],
            compiler_params=params,
            cost_estimate=pl.CostEstimate(
                flops=4 * count * block_rows * width * out_width,
                bytes_accessed=count * block_rows * width * 6,
                transcendentals=0,
            ),
            name="forward",
        )(tile_slot, tile_up, place, tokens, frozen_weight, near_down, far_down, near_up, far_up)

    def swapped(x):
        return lax.ppermute(x, "mp", swap)

    def shifted(x):
        return lax.ppermute(x, "mp", ring)

    def behind(back):
        return lambda i, p: lax.rem(p[0] - back + outer, outer)

    def first(i, p):
        return 0

    def ring_step(s, kept, near, run, c):
        at = behind(s % outer)
        coded = [(near, at)] + [(r, first) for r in run]
        return add_parts(place, block_rows, 1, (kept, at), coded, c * each, each)

    def both_step(s, kept, near, run, beside=()):
        at = behind(s % outer)
        return add_parts(place, block_rows, 1, (kept, at), [(near, at), (run, first)], 0, 2 * each, 0 if beside else None, beside)

    def pair_step(s, kept, run):
        at = behind(s)
        pick = (kept, lambda i, p: at(i, p) * inner + i)
        return add_parts(place, block_rows, inner, pick, [(r, lambda i, p: i) for r in run])

    def pair_end(kept, run, got):
        def whose(i, p):
            return p[1] if got else 1 - p[1]

        coded = [(run, whose)] + [(g, first) for g in got]
        return add_parts(place, block_rows, 1, (kept, lambda i, p: p[0] * inner + whose(i, p)), coded, last=2 * each if got else None)

    order = []
    for s in range(outer):
        at = ((my_outer - s) % outer) * inner
        order += [at + my_inner, at + other]
    cots = [cotangent, swapped(cotangent)]
    block, cots[-1], ups, cut = tie((shifted(cotangent), cots[-1], ups, cut))
    ups = jnp.concatenate(ups, axis=0)
    near_up = jnp.concatenate([ups, swapped(ups)], axis=0)
    near_down = lax.all_to_all(cut, "mp", split_axis=0, concat_axis=0, tiled=True)
    cots += [block, swapped(block)]
    if outer > 2:
        block = shifted(block)
    block, cots[-1], near_up, near_down = tie((block, cots[-1], near_up, near_down))
    far_up, far_down = (lax.ppermute(a, "dp", cores) for a in (near_up, near_down))
    own = rank // n
    half = rank // inner
    late_shrink, pair = forward(2 * each, steps - 2 * each, 0)
    shrink, kept, *sents = forward(0, 2 * each, 2)
    near, outs, runs, sums, done = {}, {}, [()] * 3, [()] * 3, [0] * 3

    def add(*chunks):
        for c in chunks:
            done[c] += 1
            if c == last:
                sums[c] = pair_step(done[c], pair, runs[c])
            else:
                sums[c] = ring_step(done[c], kept, near[c], runs[c], c)

    def send(*chunks):
        for c in chunks:
            runs[c] = (shifted(sums[c]),)

    for s in range(2, outer):
        cots += [block, swapped(block)]
        if s < outer - 1:
            block = shifted(block)
        if s == 2:
            add(last)
            block, cots[-1], sums[last] = tie((block, cots[-1], sums[last]))
    send(last)

    shrink = jnp.concatenate([shrink, late_shrink], axis=1)
    theirs = lax.dynamic_slice_in_dim(shrink, other * half, half, 0)
    mine = lax.dynamic_slice_in_dim(shrink, my_inner * half, half, 0)
    cots[-1], kept, sents, runs, mine, theirs = tie((cots[-1], kept, sents, runs, mine, theirs))
    theirs = swapped(theirs)
    add(last)
    mine += theirs
    send(last)
    cots[-1], mine = tie((cots[-1], mine))
    shrink = [lax.dynamic_slice_in_dim(mine, my_outer * own, own, 0)]
    for s in range(1, outer):
        theirs = lax.dynamic_slice_in_dim(mine, ((my_outer + s) % outer) * own, own, 0)
        shrink.append(lax.ppermute(theirs, "mp", [(i, (i + s * inner) % n) for i in range(n)]))
    near[0] = swapped(sents[0])

    if cols % 128:
        natural = jnp.stack(cots)[jnp.argsort(jnp.stack(order))]
        cots = [jnp.transpose(natural, (1, 0, 2)).reshape(rows, out_width)]
    cot_all, back, gdown, rdown = pl.pallas_call(
        functools.partial(gradient_kernel, len(cots)),
        grid_spec=pltpu.PrefetchScalarGridSpec(
            num_scalar_prefetch=3,
            grid=(steps,),
            in_specs=[strip(a.shape[1]) for a in cots]
            + [strip(width), whole(n, rank, out_width), whole(n, rank, out_width)],
            out_specs=[
                strip(out_width),
                strip(2 * rank),
                whole(n, rank, width),
                whole(n, rank, width),
            ],
            scratch_shapes=[
                pltpu.VMEM((slots, 2 * rank, out_width), BF16),
                pltpu.VMEM((block_rows, out_width), BF16),
                pltpu.VMEM((slots, rank, width), F32),
            ],
        ),
        out_shape=[
            jax.ShapeDtypeStruct((rows, out_width), BF16),
            jax.ShapeDtypeStruct((rows, 2 * rank), BF16),
            jax.ShapeDtypeStruct((n, rank, width), F32),
            jax.ShapeDtypeStruct((n, rank, width), F32),
        ],
        compiler_params=params,
        cost_estimate=pl.CostEstimate(
            flops=2 * rows * width * out_width, bytes_accessed=rows * (width * 2 + out_width * 4), transcendentals=0
        ),
        name="gradients",
    )(tile_slot, tile_up, jnp.stack(order).astype(jnp.int32), *cots, tokens, near_up, far_up)
    near[0], gdown, rdown, runs, shrink = tie((near[0], gdown, rdown, runs, shrink))
    shrink = sum(shrink[1:], shrink[0])
    near[1] = swapped(sents[1])
    add(0)
    sums, near[0] = tie((sums, near[0]))
    send(0)
    while done[last] < outer - 1:
        add(last)
        send(last)

    gup, rup = pl.pallas_call(
        up_kernel,
        grid_spec=pltpu.PrefetchScalarGridSpec(
            num_scalar_prefetch=1,
            grid=(steps,),
            in_specs=[pl.BlockSpec((own, block_rows), lambda i, s: (0, i)), strip(out_width)],
            out_specs=[whole(n, own, out_width), whole(n, own, out_width)],
            scratch_shapes=[pltpu.VMEM((slots, own, out_width), F32)],
        ),
        out_shape=[
            jax.ShapeDtypeStruct((n, own, out_width), F32),
            jax.ShapeDtypeStruct((n, own, out_width), F32),
        ],
        compiler_params=params,
        cost_estimate=pl.CostEstimate(flops=0, bytes_accessed=rows * out_width * 2, transcendentals=0),
        name="up_gradient",
    )(tile_slot, shrink, cot_all)
    rdown = lax.ppermute(rdown, "dp", cores)
    rup = lax.ppermute(rup, "dp", cores)
    packed_rows = rank + PAD
    packed = pl.pallas_call(
        pack_kernel,
        grid=(2,),
        in_specs=[
            pl.BlockSpec((n // 2, rank, width), lambda i: (i, 0, 0)),
            pl.BlockSpec((n // 2, rank, width), lambda i: (i, 0, 0)),
            pl.BlockSpec((n // 2, own, out_width), lambda i: (i, 0, 0)),
            pl.BlockSpec((n // 2, own, out_width), lambda i: (i, 0, 0)),
        ],
        out_specs=pl.BlockSpec((n // 2, packed_rows, width), lambda i: (i, 0, 0)),
        out_shape=jax.ShapeDtypeStruct((n, packed_rows, width), jnp.int16),
        compiler_params=params,
        name="pack_gradients",
    )(gdown, rdown, gup, rup)
    near, packed = tie((near, packed))
    add(1)
    send(1)
    runs, packed = tie((runs, packed))
    landed = lax.all_to_all(packed, "mp", split_axis=0, concat_axis=0, tiled=True)
    down_gradient, up_gradient = pl.pallas_call(
        functools.partial(unpack_kernel, outer),
        grid=(2,),
        in_specs=[pl.BlockSpec((n // 2, packed_rows, width), lambda i: (i, 0, 0))],
        out_specs=[
            pl.BlockSpec((1, rank, entire_width // 2), lambda i: (0, 0, i)),
            pl.BlockSpec((n, own, out_width), lambda i: (0, 0, 0)),
        ],
        out_shape=[
            jax.ShapeDtypeStruct((1, rank, entire_width), F32),
            jax.ShapeDtypeStruct((n, own, out_width), F32),
        ],
        compiler_params=params,
        name="unpack_gradients",
    )(landed)

    token_gradient = pl.pallas_call(
        token_kernel,
        grid_spec=pltpu.PrefetchScalarGridSpec(
            num_scalar_prefetch=1,
            grid=(steps,),
            in_specs=[
                strip(out_width),
                whole(width, out_width),
                whole(n, rank, width),
                whole(n, rank, width),
                strip(2 * rank),
            ],
            out_specs=strip(width),
            scratch_shapes=[pltpu.VMEM((slots, 2 * rank, width), BF16)],
        ),
        out_shape=jax.ShapeDtypeStruct((rows, width), BF16),
        compiler_params=params,
        cost_estimate=pl.CostEstimate(
            flops=3 * rows * width * out_width, bytes_accessed=rows * (width * 2 + out_width * 2), transcendentals=0
        ),
        name="token_gradient",
    )(tile_slot, cot_all, frozen_weight, near_down, far_down, back)
    run = runs[last][0]
    got = swapped(pair_end(pair, run, []))
    both = (near[0], near[1])
    run = (runs[0][0], runs[1][0])
    for s in range(2, outer):
        run = shifted(both_step(s, kept, both, run))
        if s == 2:
            got, run, token_gradient = tie((got, run, token_gradient))
            outs[last] = pair_end(pair, runs[last][0], [got])
    run, down_gradient, up_gradient, outs = tie((run, down_gradient, up_gradient, outs))
    output = both_step(outer, kept, both, run, (outs[last],))

    up_gradient = up_gradient.reshape(1, rank, out_width)
    return output, token_gradient, jnp.swapaxes(down_gradient, 1, 2), up_gradient


def solution(mesh):
    placed = (
        P(("groups", "dp"), "mp"),
        P("mp", None),
        P(("groups", "dp"), "mp"),
        P(("groups", "dp", "mp"), None, None),
        P(("groups", "dp", "mp"), None, None),
        P(("groups", "dp"), None),
        P(("groups", "dp"), None),
        P("groups"),
    )
    return jax.shard_map(
        body,
        mesh=mesh,
        in_specs=placed,
        out_specs=(
            P(("groups", "dp"), "mp"),
            P(("groups", "dp"), "mp"),
            P(("groups", "dp", "mp"), None, None),
            P(("groups", "dp", "mp"), None, None),
        ),
        check_vma=False,
    )
```
